256 devices in a mesh: tm: 4 (over x), orig: 64 (over z, y, core).
Axes of the slice: x: 4, y: 4, z: 8, core: 2. Of those that a mesh axis runs over, the one named last changes fastest.
Arguments:
- trip_counts: bfloat16 [12, 768, 256, 256], P('tm', 'orig'), may hold values from 0.25 to 4
- anchor_hour: float32 [12, 16384], P('tm', 'orig'), may hold values from 100 to 3000
- dest_hour: float32 [12, 32768], P('tm'), may hold values from 100 to 3000
- daily_target: bfloat16 [768, 256, 256], P('orig'), may hold values from 2 to 40
- block_columns: int32 [768], P('orig'), may hold values from -1 to 127, as said below
Outputs:
- fitted: bfloat16 [12, 768, 256, 256], P('tm', 'orig')
- dest_gap: float32 [12, 32768], P('tm', 'orig')
The draws below stay inside these ranges and needn't reach their ends.
Inputs may be any that keep to these rules, and one draw needn't show every extreme that they name: `block_columns`: within each anchor block row the live column numbers are distinct and come first, followed by -1 for empty slots; every block row has at least one live slot, and some block row has all 12 live.
All inputs are finite; a program needn't handle non-finite values.
Results may differ from the reference program's by a relative error of at most 0.001.
Values sent between devices are 32-bit elements; how exact they have to be, the bound alone decides.
A program may use at most 64 MiB of HBM per device.

```python
import math
import jax
import jax.numpy as jnp
from jax import lax

BLOCK = 256
ZONES = 32768
SLOTS = 12
BINS = 12
COLS = 128
ANCHORS = 16384
SLOTS_ALL = 768
N_ORIG = 64


def draw_block_columns(key, part):
    devices = SLOTS_ALL // SLOTS
    key_list = jax.random.split(key, 4)

    def one_order(row_key):
        return jax.random.permutation(row_key, COLS)
    orders = jax.vmap(one_order)(jax.random.split(key_list[0], devices))[:, :SLOTS]
    small_count = 1 + jax.random.randint(key_list[1], (devices,), 0, max(SLOTS // 2, 1))
    full_draw = jax.random.randint(key_list[2], (devices,), 0, 8)
    chosen_device = jax.random.randint(key_list[3], (), 0, devices)
    counts = jnp.where((full_draw == 0) | (jnp.arange(devices) == chosen_device), SLOTS, small_count)
    slot_index = jnp.arange(SLOTS)[None, :]
    return jnp.where(slot_index < counts[:, None], orders, -1).astype(jnp.int32).reshape(-1)


def levels(key, extent, cuts, smallest, largest):
    def one(dim, shards_of):
        heights = jax.random.uniform(jax.random.fold_in(jax.random.fold_in(key, 6), dim), (shards_of,), jnp.float32, smallest / len(cuts), largest / len(cuts))
        return jnp.repeat(jnp.exp(heights), extent[dim] // shards_of).reshape((-1,) + (1,) * (len(extent) - dim - 1))

    level = one(*cuts[0])
    for cut in cuts[1:]:
        level = level * one(*cut)
    return level


def setup_inputs(seed: int = 0) -> dict:
    streams_of = jax.random.split(jax.random.key(seed), 6)
    trip_counts = jnp.clip(jnp.exp(math.log(4.0) - 2.7725887 * jax.random.uniform(streams_of[0], (BINS, SLOTS_ALL, BLOCK, BLOCK), jnp.float32) ** levels(streams_of[0], (BINS, SLOTS_ALL, BLOCK, BLOCK), ((0, 4), (1, 64)), -0.2, 0.2)), 0.25, 4.0).astype(jnp.bfloat16)
    anchor_hour = jnp.clip(jnp.exp(math.log(3000.0) - 3.4011974 * jax.random.uniform(streams_of[1], (BINS, ANCHORS), jnp.float32) ** levels(streams_of[1], (BINS, ANCHORS), ((0, 4), (1, 64)), -0.2, 0.2)), 100.0, 3000.0)
    dest_hour = jnp.clip(jnp.exp(math.log(3000.0) - 3.4011974 * jax.random.uniform(streams_of[2], (BINS, ZONES), jnp.float32) ** levels(streams_of[2], (BINS, ZONES), ((0, 4),), -0.2, 0.2)), 100.0, 3000.0)
    daily_target = jnp.clip(jnp.exp(math.log(40.0) - 2.9957323 * jax.random.uniform(streams_of[3], (SLOTS_ALL, BLOCK, BLOCK), jnp.float32) ** levels(streams_of[3], (SLOTS_ALL, BLOCK, BLOCK), ((0, 64),), -0.2, 0.2)), 2.0, 40.0).astype(jnp.bfloat16)
    block_columns = draw_block_columns(jax.random.fold_in(streams_of[5], 71), 0)
    return dict(trip_counts=trip_counts, anchor_hour=anchor_hour, dest_hour=dest_hour, daily_target=daily_target, block_columns=block_columns)


def anchor_scaled(trip_block, anchor_block, live_mask):
    values = trip_block.astype(jnp.float32) * live_mask[None, :, None, None]
    row_sums = jnp.sum(values, axis=(1, 3))
    return values * (anchor_block / row_sums)[:, None, :, None]


def column_sums(values, onehot):
    return jnp.einsum("tsj,sc->tcj", jnp.sum(values, axis=2), onehot, precision=lax.Precision.HIGHEST)


def reference(trip_counts, anchor_hour, dest_hour, daily_target, block_columns):
    shaped = trip_counts.reshape(BINS, N_ORIG, SLOTS, BLOCK, BLOCK)
    columns = block_columns.reshape(N_ORIG, SLOTS)
    anchors = anchor_hour.reshape(BINS, N_ORIG, BLOCK)
    targets = daily_target.reshape(N_ORIG, SLOTS, BLOCK, BLOCK)

    def pieces(index):
        column_row = lax.dynamic_index_in_dim(columns, index, 0, keepdims=False)
        live_mask = (column_row >= 0).astype(jnp.float32)
        onehot = (column_row[:, None] == jnp.arange(COLS, dtype=jnp.int32)[None, :]).astype(jnp.float32)
        trip_block = lax.dynamic_index_in_dim(shaped, index, 1, keepdims=False)
        anchor_block = lax.dynamic_index_in_dim(anchors, index, 1, keepdims=False)
        return anchor_scaled(trip_block, anchor_block, live_mask), live_mask, onehot

    def first_pass(index, totals):
        anchor_fit, live_mask, onehot = pieces(index)
        return totals + column_sums(anchor_fit, onehot)

    zeros = jnp.zeros((BINS, COLS, BLOCK), jnp.float32)
    totals = lax.fori_loop(0, N_ORIG, first_pass, zeros)
    dest_gain = dest_hour.reshape(BINS, COLS, BLOCK) / jnp.maximum(totals, 1.0)

    def second_pass(index, state):
        fitted, after = state
        anchor_fit, live_mask, onehot = pieces(index)
        spread = jnp.einsum("sc,tcj->tsj", onehot, dest_gain, precision=lax.Precision.HIGHEST)
        dest_fit = anchor_fit * spread[:, :, None, :]
        daily_sum = jnp.sum(dest_fit, axis=0)
        target_block = lax.dynamic_index_in_dim(targets, index, 0, keepdims=False).astype(jnp.float32)
        daily_fit = dest_fit * (target_block / (daily_sum + 1.0 - live_mask[:, None, None]))[None]
        fitted = lax.dynamic_update_index_in_dim(fitted, daily_fit.astype(jnp.bfloat16), index, 1)
        return fitted, after + column_sums(daily_fit, onehot)

    fitted, after = lax.fori_loop(0, N_ORIG, second_pass, (jnp.zeros_like(shaped), zeros))
    dest_gap = after.reshape(BINS, ZONES) / dest_hour - 1.0
    return fitted.reshape(BINS, SLOTS_ALL, BLOCK, BLOCK), dest_gap
```

```python
import jax
import jax.numpy as jnp
from jax import lax
from jax.experimental import pallas as pl
from jax.experimental.pallas import tpu as pltpu
from jax.sharding import PartitionSpec as P

BINS = 3
SLOTS = 12
SIDE = 256
LANES = 128
GROUP = 8
DEPTH = 8
PIECE = DEPTH * BINS * 2
KEYS = 128
ROWS = 64
F32 = jnp.float32


def send(src, dst, send_sem, recv_sem, tm, orig):
    return pltpu.make_async_remote_copy(
        src_ref=src,
        dst_ref=dst,
        send_sem=send_sem,
        recv_sem=recv_sem,
        device_id=(tm, orig),
        device_id_type=pl.DeviceIdType.MESH,
    )


def kernel(
    cols_ref, keys_ref, anchor_ref, trips_ref, dest_ref, target_ref,
    fitted_ref, gap_ref,
    trips, part, factor, half_in, quarter_in, target, row_acc, anchor_fit, dest_row, dest8,
    onehot, sums, spread, gains, wide, wide_in, narrow, narrow_in, gain_z, gain_piece,
    wide2, wide2_in, narrow2, narrow2_in,
    trips_sem, target_sem, dest_sem, fitted_sem,
    half_s, half_r, quarter_s, quarter_r, back_s, back_r, whole_s, whole_r,
    wide_s, wide_r, narrow_s, narrow_r, gz_s, gz_r, gg_s, gg_r, wide2_s, wide2_r, narrow2_s, narrow2_r,
):
    x = lax.axis_index("tm")
    q = lax.axis_index("orig")
    z, g = q // GROUP, q % GROUP
    v = x // 2
    u = (x + v) % 2
    pa = x + 1 - 2 * (x % 2)
    pb = 3 - x
    group = [z * GROUP + (g + d) % GROUP for d in range(1, GROUP)]
    column = [((z + d) % DEPTH) * GROUP + g for d in range(1, DEPTH)]

    barrier = pltpu.get_barrier_semaphore()
    partners = [(x, o) for o in group + column] + [(pa, q), (pb, q)]
    for t_, o_ in partners:
        pl.semaphore_signal(barrier, inc=1, device_id=(t_, o_), device_id_type=pl.DeviceIdType.MESH)

    first, second = (pa, pb), (pb, pa)
    keep1, keep2 = (u, v), (v, u)
    kept64 = [pl.multiple_of(128 * h + 64 * keep1[h], 64) for h in range(2)]
    sent64 = [pl.multiple_of(128 * h + 64 * (1 - keep1[h]), 64) for h in range(2)]
    kept32 = [pl.multiple_of(kept64[h] + 32 * keep2[h], 32) for h in range(2)]
    sent32 = [pl.multiple_of(kept64[h] + 32 * (1 - keep2[h]), 32) for h in range(2)]

    def load_trips(s):
        return pltpu.make_async_copy(trips_ref.at[:, s], trips.at[s], trips_sem.at[s])

    def load_target(h):
        return pltpu.make_async_copy(
            target_ref.at[:, pl.ds(kept32[h], 32), :], target.at[h], target_sem.at[h]
        )

    load_dest = pltpu.make_async_copy(
        dest_ref.at[:, pl.ds(pl.multiple_of(q * 512, 512), 512)], dest_row, dest_sem
    )

    @pl.loop(0, SLOTS)
    def _(s):
        load_trips(s).start()

    load_dest.start()
    for h in range(2):
        load_target(h).start()

    r = lax.broadcasted_iota(jnp.int32, (GROUP * PIECE, KEYS), 0)
    rg = (r * 1366) >> 16
    rem = r - rg * 48
    rz = (rem * 10923) >> 16
    rem = rem - rz * 6
    row_key = (16 * rz + 2 * rg + (rem & 1)) * BINS + (rem >> 1)
    onehot[...] = jnp.where(row_key == keys_ref[...], 1.0, 0.0).astype(F32)

    diagonal = lax.broadcasted_iota(jnp.int32, (SIDE, SIDE), 0) == lax.broadcasted_iota(
        jnp.int32, (SIDE, SIDE), 1
    )
    row_acc[...] = jnp.zeros_like(row_acc)
    sums[...] = jnp.zeros_like(sums)
    narrow[...] = jnp.zeros_like(narrow)
    narrow2[...] = jnp.zeros_like(narrow2)
    dest8[...] = jnp.ones_like(dest8)

    @pl.loop(0, SLOTS)
    def _(s):
        load_trips(s).wait()
        live = jnp.where(cols_ref[s] >= 0, 1.0, 0.0).astype(F32)
        for t in range(BINS):
            for c in range(SIDE // ROWS):
                rows = pl.ds(c * ROWS, ROWS)
                left = trips[s, t, rows, pl.ds(0, LANES)].astype(F32)
                right = trips[s, t, rows, pl.ds(LANES, LANES)].astype(F32)
                row_acc[t, rows, :] += (left + right) * live

    for t in range(BINS):
        hour = jnp.sum(jnp.where(diagonal, anchor_ref[pl.ds(t, 1), :], 0.0), axis=1, keepdims=True)
        total = jnp.sum(row_acc[t], axis=1, keepdims=True)
        anchor_fit[t] = jnp.broadcast_to(hour / total, (SIDE, LANES))

    @pl.loop(0, SLOTS)
    def _(s):
        for t in range(BINS):
            for l in range(SIDE // LANES):
                lanes = pl.ds(l * LANES, LANES)
                acc = jnp.zeros((ROWS, LANES), F32)
                for c in range(SIDE // ROWS):
                    rows = pl.ds(c * ROWS, ROWS)
                    acc += trips[s, t, rows, lanes].astype(F32) * anchor_fit[t, rows, :]
                sums[s, pl.ds(t, 1), lanes] = jnp.sum(acc, axis=0, keepdims=True)

    pl.semaphore_wait(barrier, len(partners))

    def owner_sums(wide, wide_in, narrow, narrow_in, wide_s, wide_r, narrow_s, narrow_r):
        wide[...] = jnp.dot(
            onehot[...], sums[...].reshape(KEYS, SIDE), precision=lax.Precision.HIGHEST, preferred_element_type=F32
        )
        copies = []
        for d in range(1, GROUP):
            other = pl.multiple_of(((g + d) % GROUP) * PIECE, PIECE)
            copies.append(
                send(wide.at[pl.ds(other, PIECE), :], wide_in.at[d - 1], wide_s.at[d - 1], wide_r.at[d - 1], x, group[d - 1])
            )
            copies[-1].start()
        total = wide[pl.ds(pl.multiple_of(g * PIECE, PIECE), PIECE), :]
        for d in range(1, GROUP):
            copies[d - 1].wait_recv()
            total = total + wide_in[d - 1]
        for c in range(DEPTH):
            narrow[c, pl.ds(0, 6), :] = total[6 * c : 6 * c + 6, :]
        more = []
        for d in range(1, DEPTH):
            more.append(
                send(narrow.at[(z + d) % DEPTH], narrow_in.at[d - 1], narrow_s.at[d - 1], narrow_r.at[d - 1], x, column[d - 1])
            )
            more[-1].start()
        total = narrow[z]
        for d in range(1, DEPTH):
            more[d - 1].wait_recv()
            total = total + narrow_in[d - 1]
        return total, copies + more

    load_dest.wait()
    for t in range(BINS):
        for b in range(2):
            dest8[pl.ds(2 * t + b, 1), :] = dest_row[pl.ds(t, 1), pl.ds(b * SIDE, SIDE)]

    total, pending = owner_sums(wide, wide_in, narrow, narrow_in, wide_s, wide_r, narrow_s, narrow_r)
    gain_z[z] = dest8[...] / jnp.maximum(total, 1.0)
    copies = []
    for d in range(1, DEPTH):
        copies.append(send(gain_z.at[z], gain_z.at[z], gz_s.at[d - 1], gz_r.at[d - 1], x, column[d - 1]))
        copies[-1].start()
    for copy in copies:
        copy.wait_recv()
    pending += copies
    for c in range(DEPTH):
        gain_piece[pl.ds(6 * c, 6), :] = gain_z[c, pl.ds(0, 6), :]
    mine = pl.ds(pl.multiple_of(g * PIECE, PIECE), PIECE)
    copies = []
    for d in range(1, GROUP):
        copies.append(send(gain_piece, gains.at[mine, :], gg_s.at[d - 1], gg_r.at[d - 1], x, group[d - 1]))
        copies[-1].start()
    gains[mine, :] = gain_piece[...]
    for copy in copies:
        copy.wait_recv()
    pending += copies
    spread[...] = lax.dot_general(
        onehot[...], gains[...], (((0,), (0,)), ((), ())),
        precision=lax.Precision.HIGHEST, preferred_element_type=F32,
    ).reshape(KEYS // 8, 8, SIDE)
    for h in range(2):
        load_target(h).wait()

    def halves(s, h):
        return send(
            part.at[s, pl.ds(sent64[h], 64), :], half_in.at[s, h], half_s.at[s, h], half_r.at[s, h], first[h], q
        )

    def quarters(s, h):
        return send(
            part.at[s, pl.ds(sent32[h], 32), :], quarter_in.at[s, h], quarter_s.at[s, h], quarter_r.at[s, h], second[h], q
        )

    def back(s, h):
        rows = pl.ds(kept32[h], 32)
        return send(factor.at[s, rows, :], factor.at[s, rows, :], back_s.at[s, h], back_r.at[s, h], second[h], q)

    def whole(s, h):
        rows = pl.ds(kept64[h], 64)
        return send(factor.at[s, rows, :], factor.at[s, rows, :], whole_s.at[s, h], whole_r.at[s, h], first[h], q)

    def store_fitted(s):
        return pltpu.make_async_copy(trips.at[s], fitted_ref.at[:, s], fitted_sem.at[s])

    @pl.loop(0, SLOTS + 4)
    def _(k):
        @pl.when(k < SLOTS)
        def _():
            s = k
            for l in range(SIDE // LANES):
                lanes = pl.ds(l * LANES, LANES)
                gain = [spread[s, pl.ds(t, 1), lanes] for t in range(BINS)]
                for c in range(SIDE // ROWS):
                    rows = pl.ds(c * ROWS, ROWS)
                    acc = jnp.zeros((ROWS, LANES), F32)
                    for t in range(BINS):
                        acc += trips[s, t, rows, lanes].astype(F32) * anchor_fit[t, rows, :] * gain[t]
                    part[s, rows, lanes] = acc
            for h in range(2):
                halves(s, h).start()

        @pl.when((k >= 1) & (k < SLOTS + 1))
        def _():
            s = k - 1
            for h in range(2):
                halves(s, h).wait_recv()
                part[s, pl.ds(kept64[h], 64), :] += half_in[s, h]
                quarters(s, h).start()

        @pl.when((k >= 2) & (k < SLOTS + 2))
        def _():
            s = k - 2
            dead = jnp.where(cols_ref[s] >= 0, 0.0, 1.0).astype(F32)
            for h in range(2):
                quarters(s, h).wait_recv()
                rows = pl.ds(kept32[h], 32)
                daily = part[s, rows, :] + quarter_in[s, h]
                factor[s, rows, :] = target[h, s].astype(F32) / (daily + dead)
                back(s, h).start()

        @pl.when((k >= 3) & (k < SLOTS + 3))
        def _():
            s = k - 3
            for h in range(2):
                back(s, h).wait_recv()
                whole(s, h).start()

        @pl.when(k >= 4)
        def _():
            s = k - 4
            for h in range(2):
                whole(s, h).wait_recv()
            for t in range(BINS):
                for l in range(SIDE // LANES):
                    lanes = pl.ds(l * LANES, LANES)
                    gain = spread[s, pl.ds(t, 1), lanes]
                    acc = jnp.zeros((ROWS, LANES), F32)
                    for c in range(SIDE // ROWS):
                        rows = pl.ds(c * ROWS, ROWS)
                        value = trips[s, t, rows, lanes].astype(F32) * anchor_fit[t, rows, :] * factor[s, rows, lanes]
                        acc += value
                        trips[s, t, rows, lanes] = (value * gain).astype(jnp.bfloat16)
                    sums[s, pl.ds(t, 1), lanes] = jnp.sum(acc, axis=0, keepdims=True) * gain
            store_fitted(s).start()

    total, more = owner_sums(wide2, wide2_in, narrow2, narrow2_in, wide2_s, wide2_r, narrow2_s, narrow2_r)
    pending += more
    gap = total / dest8[...] - 1.0
    for t in range(BINS):
        for b in range(2):
            gap_ref[pl.ds(t, 1), pl.ds(b * SIDE, SIDE)] = gap[2 * t + b : 2 * t + b + 1, :]

    for copy in pending:
        copy.wait_send()

    @pl.loop(0, SLOTS)
    def _(s):
        for h in range(2):
            halves(s, h).wait_send()
            quarters(s, h).wait_send()
            back(s, h).wait_send()
            whole(s, h).wait_send()
        store_fitted(s).wait()


def on_device(trip_counts, anchor_hour, dest_hour, daily_target, block_columns):
    bins = jnp.arange(8, dtype=jnp.int32)[None, :]
    keys = jnp.where(
        (block_columns[:, None] >= 0) & (bins < BINS), block_columns[:, None] * BINS + bins, -1
    ).reshape(1, SLOTS * 8)
    keys = jnp.pad(keys, ((0, 0), (0, KEYS - SLOTS * 8)), constant_values=-1)
    vmem = lambda *shape: pltpu.VMEM(shape, F32)
    dma = lambda *shape: pltpu.SemaphoreType.DMA(shape)
    scratch = [
        pltpu.VMEM((SLOTS, BINS, SIDE, SIDE), jnp.bfloat16),
        vmem(SLOTS, SIDE, SIDE),
        vmem(SLOTS, SIDE, SIDE),
        vmem(SLOTS, 2, 64, SIDE),
        vmem(SLOTS, 2, 32, SIDE),
        pltpu.VMEM((2, SLOTS, 32, SIDE), jnp.bfloat16),
        vmem(BINS, SIDE, LANES),
        vmem(BINS, SIDE, LANES),
        vmem(BINS, 512),
        vmem(8, SIDE),
        vmem(GROUP * PIECE, KEYS),
        vmem(KEYS // 8, 8, SIDE),
        vmem(KEYS // 8, 8, SIDE),
        vmem(GROUP * PIECE, SIDE),
        vmem(GROUP * PIECE, SIDE),
        vmem(GROUP - 1, PIECE, SIDE),
        vmem(DEPTH, 8, SIDE),
        vmem(DEPTH - 1, 8, SIDE),
        vmem(DEPTH, 8, SIDE),
        vmem(PIECE, SIDE),
        vmem(GROUP * PIECE, SIDE),
        vmem(GROUP - 1, PIECE, SIDE),
        vmem(DEPTH, 8, SIDE),
        vmem(DEPTH - 1, 8, SIDE),
        dma(SLOTS), dma(2), pltpu.SemaphoreType.DMA, dma(SLOTS),
    ] + [dma(SLOTS, 2)] * 8 + [dma(7)] * 12
    fitted, gap = pl.pallas_call(
        kernel,
        out_shape=(
            jax.ShapeDtypeStruct(trip_counts.shape, jnp.bfloat16),
            jax.ShapeDtypeStruct((BINS, 512), F32),
        ),
        in_specs=[
            pl.BlockSpec(memory_space=pltpu.SMEM),
            pl.BlockSpec(memory_space=pltpu.VMEM),
            pl.BlockSpec(memory_space=pltpu.VMEM),
            pl.BlockSpec(memory_space=pl.ANY),
            pl.BlockSpec(memory_space=pl.ANY),
            pl.BlockSpec(memory_space=pl.ANY),
        ],
        out_specs=(pl.BlockSpec(memory_space=pl.ANY), pl.BlockSpec(memory_space=pltpu.VMEM)),
        scratch_shapes=scratch,
        compiler_params=pltpu.CompilerParams(
            collective_id=0, has_side_effects=True, vmem_limit_bytes=40 * 1024 * 1024
        ),
        cost_estimate=pl.CostEstimate(flops=40_000_000, bytes_accessed=11_000_000, transcendentals=0),
    )(block_columns, keys, anchor_hour, trip_counts, dest_hour, daily_target)
    return fitted, gap


def solution(mesh):
    placed = (
        P("tm", "orig", None, None),
        P("tm", "orig"),
        P("tm", None),
        P("orig", None, None),
        P("orig"),
    )
    return jax.shard_map(
        on_device,
        mesh=mesh,
        in_specs=placed,
        out_specs=(P("tm", "orig", None, None), P("tm", "orig")),
        check_vma=False,
    )
```

```python
import jax
import jax.numpy as jnp
from jax import lax
from jax.experimental import pallas as pl
from jax.experimental.pallas import tpu as pltpu
from jax.sharding import PartitionSpec as P

BINS = 3
SLOTS = 12
SIDE = 256
LANES = 128
GROUP = 8
DEPTH = 8
PIECE = DEPTH * BINS * 2
KEYS = 128
ROWS = 64
LAG = 2
F32 = jnp.float32


def send(src, dst, send_sem, recv_sem, tm, orig):
    return pltpu.make_async_remote_copy(
        src_ref=src,
        dst_ref=dst,
        send_sem=send_sem,
        recv_sem=recv_sem,
        device_id=(tm, orig),
        device_id_type=pl.DeviceIdType.MESH,
    )


def kernel(
    cols_ref, anchor_ref, trips_ref, dest_ref, target_ref,
    fitted_ref, gap_ref,
    trips, part, factor, half_in, quarter_in, target, row_acc, anchor_fit, dest_row, dest8,
    onehot, sums, spread, gains, wide, wide_in, narrow, narrow_in, gain_z, gain_piece,
    wide2, wide2_in, narrow2, narrow2_in,
    trips_sem, target_sem, dest_sem, fitted_sem,
    half_s, half_r, quarter_s, quarter_r, back_s, back_r, whole_s, whole_r,
    wide_s, wide_r, narrow_s, narrow_r, gz_s, gz_r, gg_s, gg_r, wide2_s, wide2_r, narrow2_s, narrow2_r,
):
    x = lax.axis_index("tm")
    q = lax.axis_index("orig")
    z, g = q // GROUP, q % GROUP
    v = x // 2
    u = (x + v) % 2
    pa = x + 1 - 2 * (x % 2)
    pb = 3 - x
    group = [z * GROUP + (g + d) % GROUP for d in range(1, GROUP)]
    column = [((z + d) % DEPTH) * GROUP + g for d in range(1, DEPTH)]

    barrier = pltpu.get_barrier_semaphore()
    partners = [(x, o) for o in group + column] + [(pa, q), (pb, q)]
    for t_, o_ in partners:
        pl.semaphore_signal(barrier, inc=1, device_id=(t_, o_), device_id_type=pl.DeviceIdType.MESH)

    first, second = (pa, pb), (pb, pa)
    keep1, keep2 = (u, v), (v, u)
    kept64 = [pl.multiple_of(128 * h + 64 * keep1[h], 64) for h in range(2)]
    sent64 = [pl.multiple_of(128 * h + 64 * (1 - keep1[h]), 64) for h in range(2)]
    kept32 = [pl.multiple_of(kept64[h] + 32 * keep2[h], 32) for h in range(2)]
    sent32 = [pl.multiple_of(kept64[h] + 32 * (1 - keep2[h]), 32) for h in range(2)]

    def load_trips(s):
        return pltpu.make_async_copy(trips_ref.at[:, s], trips.at[s], trips_sem.at[s])

    def load_target(h):
        return pltpu.make_async_copy(
            target_ref.at[:, pl.ds(kept32[h], 32), :], target.at[h], target_sem.at[h]
        )

    load_dest = pltpu.make_async_copy(
        dest_ref.at[:, pl.ds(pl.multiple_of(q * 512, 512), 512)], dest_row, dest_sem
    )

    @pl.loop(0, SLOTS)
    def _(s):
        load_trips(s).start()

    load_dest.start()
    for h in range(2):
        load_target(h).start()

    r = lax.broadcasted_iota(jnp.int32, (GROUP * PIECE, KEYS), 0)
    rg = (r * 1366) >> 16
    rem = r - rg * 48
    rz = (rem * 10923) >> 16
    rem = rem - rz * 6
    row_key = (16 * rz + 2 * rg + (rem & 1)) * BINS + (rem >> 1)
    lane = lax.broadcasted_iota(jnp.int32, (1, KEYS), 1)
    key = jnp.full((1, KEYS), -1, jnp.int32)
    for s in range(SLOTS):
        col = cols_ref[s]
        in_slot = (lane >= 8 * s) & (lane < 8 * s + BINS) & (jnp.full((1, KEYS), col, jnp.int32) >= 0)
        key = jnp.where(in_slot, col * BINS + lane - 8 * s, key)
    onehot[...] = jnp.where(row_key == key, 1.0, 0.0).astype(F32)

    diagonal = lax.broadcasted_iota(jnp.int32, (SIDE, SIDE), 0) == lax.broadcasted_iota(
        jnp.int32, (SIDE, SIDE), 1
    )
    row_acc[...] = jnp.zeros_like(row_acc)
    sums[...] = jnp.zeros_like(sums)
    narrow[...] = jnp.zeros_like(narrow)
    narrow2[...] = jnp.zeros_like(narrow2)
    dest8[...] = jnp.ones_like(dest8)

    @pl.loop(0, SLOTS)
    def _(s):
        load_trips(s).wait()
        live = jnp.where(cols_ref[s] >= 0, 1.0, 0.0).astype(F32)
        for t in range(BINS):
            for c in range(SIDE // ROWS):
                rows = pl.ds(c * ROWS, ROWS)
                left = trips[s, t, rows, pl.ds(0, LANES)].astype(F32)
                right = trips[s, t, rows, pl.ds(LANES, LANES)].astype(F32)
                row_acc[t, rows, :] += (left + right) * live

    for t in range(BINS):
        hour = jnp.sum(jnp.where(diagonal, anchor_ref[pl.ds(t, 1), :], 0.0), axis=1, keepdims=True)
        total = jnp.sum(row_acc[t], axis=1, keepdims=True)
        anchor_fit[t] = jnp.broadcast_to(hour / total, (SIDE, LANES))

    @pl.loop(0, SLOTS)
    def _(s):
        for t in range(BINS):
            for l in range(SIDE // LANES):
                lanes = pl.ds(l * LANES, LANES)
                acc = jnp.zeros((ROWS, LANES), F32)
                for c in range(SIDE // ROWS):
                    rows = pl.ds(c * ROWS, ROWS)
                    acc += trips[s, t, rows, lanes].astype(F32) * anchor_fit[t, rows, :]
                sums[s, pl.ds(t, 1), lanes] = jnp.sum(acc, axis=0, keepdims=True)

    pl.semaphore_wait(barrier, len(partners))

    def owner_sums(wide, wide_in, narrow, narrow_in, wide_s, wide_r, narrow_s, narrow_r):
        wide[...] = jnp.dot(
            onehot[...], sums[...].reshape(KEYS, SIDE), precision=lax.Precision.HIGHEST, preferred_element_type=F32
        )
        copies = []
        for d in range(1, GROUP):
            other = pl.multiple_of(((g + d) % GROUP) * PIECE, PIECE)
            copies.append(
                send(wide.at[pl.ds(other, PIECE), :], wide_in.at[d - 1], wide_s.at[d - 1], wide_r.at[d - 1], x, group[d - 1])
            )
            copies[-1].start()
        total = wide[pl.ds(pl.multiple_of(g * PIECE, PIECE), PIECE), :]
        for d in range(1, GROUP):
            copies[d - 1].wait_recv()
            total = total + wide_in[d - 1]
        for c in range(DEPTH):
            narrow[c, pl.ds(0, 6), :] = total[6 * c : 6 * c + 6, :]
        more = []
        for d in range(1, DEPTH):
            more.append(
                send(narrow.at[(z + d) % DEPTH], narrow_in.at[d - 1], narrow_s.at[d - 1], narrow_r.at[d - 1], x, column[d - 1])
            )
            more[-1].start()
        total = narrow[z]
        for d in range(1, DEPTH):
            more[d - 1].wait_recv()
            total = total + narrow_in[d - 1]
        return total, copies + more

    load_dest.wait()
    for t in range(BINS):
        for b in range(2):
            dest8[pl.ds(2 * t + b, 1), :] = dest_row[pl.ds(t, 1), pl.ds(b * SIDE, SIDE)]

    total, pending = owner_sums(wide, wide_in, narrow, narrow_in, wide_s, wide_r, narrow_s, narrow_r)
    gain_z[z] = dest8[...] / jnp.maximum(total, 1.0)
    copies = []
    for d in range(1, DEPTH):
        copies.append(send(gain_z.at[z], gain_z.at[z], gz_s.at[d - 1], gz_r.at[d - 1], x, column[d - 1]))
        copies[-1].start()
    for copy in copies:
        copy.wait_recv()
    pending += copies
    for c in range(DEPTH):
        gain_piece[pl.ds(6 * c, 6), :] = gain_z[c, pl.ds(0, 6), :]
    mine = pl.ds(pl.multiple_of(g * PIECE, PIECE), PIECE)
    copies = []
    for d in range(1, GROUP):
        copies.append(send(gain_piece, gains.at[mine, :], gg_s.at[d - 1], gg_r.at[d - 1], x, group[d - 1]))
        copies[-1].start()
    gains[mine, :] = gain_piece[...]
    for copy in copies:
        copy.wait_recv()
    pending += copies
    spread[...] = lax.dot_general(
        onehot[...], gains[...], (((0,), (0,)), ((), ())),
        precision=lax.Precision.HIGHEST, preferred_element_type=F32,
    ).reshape(KEYS // 8, 8, SIDE)
    for h in range(2):
        load_target(h).wait()

    def halves(s, h):
        return send(
            part.at[s, pl.ds(sent64[h], 64), :], half_in.at[s, h], half_s.at[s, h], half_r.at[s, h], first[h], q
        )

    def quarters(s, h):
        return send(
            part.at[s, pl.ds(sent32[h], 32), :], quarter_in.at[s, h], quarter_s.at[s, h], quarter_r.at[s, h], second[h], q
        )

    def back(s, h):
        rows = pl.ds(kept32[h], 32)
        return send(factor.at[s, rows, :], factor.at[s, rows, :], back_s.at[s, h], back_r.at[s, h], second[h], q)

    def whole(s, h):
        rows = pl.ds(kept64[h], 64)
        return send(factor.at[s, rows, :], factor.at[s, rows, :], whole_s.at[s, h], whole_r.at[s, h], first[h], q)

    def store_fitted(s):
        return pltpu.make_async_copy(trips.at[s], fitted_ref.at[:, s], fitted_sem.at[s])

    @pl.loop(0, SLOTS + 4 * LAG)
    def _(k):
        @pl.when(k < SLOTS)
        def _():
            s = k
            for l in range(SIDE // LANES):
                lanes = pl.ds(l * LANES, LANES)
                gain = [spread[s, pl.ds(t, 1), lanes] for t in range(BINS)]
                for c in range(SIDE // ROWS):
                    rows = pl.ds(c * ROWS, ROWS)
                    acc = jnp.zeros((ROWS, LANES), F32)
                    for t in range(BINS):
                        acc += trips[s, t, rows, lanes].astype(F32) * anchor_fit[t, rows, :] * gain[t]
                    part[s, rows, lanes] = acc
            for h in range(2):
                halves(s, h).start()

        @pl.when((k >= LAG) & (k < SLOTS + LAG))
        def _():
            s = k - LAG
            for h in range(2):
                halves(s, h).wait_recv()
                part[s, pl.ds(kept64[h], 64), :] += half_in[s, h]
                quarters(s, h).start()

        @pl.when((k >= 2 * LAG) & (k < SLOTS + 2 * LAG))
        def _():
            s = k - 2 * LAG
            dead = jnp.where(cols_ref[s] >= 0, 0.0, 1.0).astype(F32)
            for h in range(2):
                quarters(s, h).wait_recv()
                rows = pl.ds(kept32[h], 32)
                daily = part[s, rows, :] + quarter_in[s, h]
                factor[s, rows, :] = target[h, s].astype(F32) / (daily + dead)
                back(s, h).start()

        @pl.when((k >= 3 * LAG) & (k < SLOTS + 3 * LAG))
        def _():
            s = k - 3 * LAG
            for h in range(2):
                back(s, h).wait_recv()
                whole(s, h).start()

        @pl.when(k >= 4 * LAG)
        def _():
            s = k - 4 * LAG
            for h in range(2):
                whole(s, h).wait_recv()
            for t in range(BINS):
                for l in range(SIDE // LANES):
                    lanes = pl.ds(l * LANES, LANES)
                    gain = spread[s, pl.ds(t, 1), lanes]
                    acc = jnp.zeros((ROWS, LANES), F32)
                    for c in range(SIDE // ROWS):
                        rows = pl.ds(c * ROWS, ROWS)
                        value = trips[s, t, rows, lanes].astype(F32) * anchor_fit[t, rows, :] * factor[s, rows, lanes]
                        acc += value
                        trips[s, t, rows, lanes] = (value * gain).astype(jnp.bfloat16)
                    sums[s, pl.ds(t, 1), lanes] = jnp.sum(acc, axis=0, keepdims=True) * gain
            store_fitted(s).start()

    total, more = owner_sums(wide2, wide2_in, narrow2, narrow2_in, wide2_s, wide2_r, narrow2_s, narrow2_r)
    pending += more
    gap = total / dest8[...] - 1.0
    for t in range(BINS):
        for b in range(2):
            gap_ref[pl.ds(t, 1), pl.ds(b * SIDE, SIDE)] = gap[2 * t + b : 2 * t + b + 1, :]

    for copy in pending:
        copy.wait_send()

    @pl.loop(0, SLOTS)
    def _(s):
        for h in range(2):
            halves(s, h).wait_send()
            quarters(s, h).wait_send()
            back(s, h).wait_send()
            whole(s, h).wait_send()
        store_fitted(s).wait()


def on_device(trip_counts, anchor_hour, dest_hour, daily_target, block_columns):
    vmem = lambda *shape: pltpu.VMEM(shape, F32)
    dma = lambda *shape: pltpu.SemaphoreType.DMA(shape)
    scratch = [
        pltpu.VMEM((SLOTS, BINS, SIDE, SIDE), jnp.bfloat16),
        vmem(SLOTS, SIDE, SIDE),
        vmem(SLOTS, SIDE, SIDE),
        vmem(SLOTS, 2, 64, SIDE),
        vmem(SLOTS, 2, 32, SIDE),
        pltpu.VMEM((2, SLOTS, 32, SIDE), jnp.bfloat16),
        vmem(BINS, SIDE, LANES),
        vmem(BINS, SIDE, LANES),
        vmem(BINS, 512),
        vmem(8, SIDE),
        vmem(GROUP * PIECE, KEYS),
        vmem(KEYS // 8, 8, SIDE),
        vmem(KEYS // 8, 8, SIDE),
        vmem(GROUP * PIECE, SIDE),
        vmem(GROUP * PIECE, SIDE),
        vmem(GROUP - 1, PIECE, SIDE),
        vmem(DEPTH, 8, SIDE),
        vmem(DEPTH - 1, 8, SIDE),
        vmem(DEPTH, 8, SIDE),
        vmem(PIECE, SIDE),
        vmem(GROUP * PIECE, SIDE),
        vmem(GROUP - 1, PIECE, SIDE),
        vmem(DEPTH, 8, SIDE),
        vmem(DEPTH - 1, 8, SIDE),
        dma(SLOTS), dma(2), pltpu.SemaphoreType.DMA, dma(SLOTS),
    ] + [dma(SLOTS, 2)] * 8 + [dma(7)] * 12
    fitted, gap = pl.pallas_call(
        kernel,
        out_shape=(
            jax.ShapeDtypeStruct(trip_counts.shape, jnp.bfloat16),
            jax.ShapeDtypeStruct((BINS, 512), F32),
        ),
        in_specs=[
            pl.BlockSpec(memory_space=pltpu.SMEM),
            pl.BlockSpec(memory_space=pltpu.VMEM),
            pl.BlockSpec(memory_space=pl.ANY),
            pl.BlockSpec(memory_space=pl.ANY),
            pl.BlockSpec(memory_space=pl.ANY),
        ],
        out_specs=(pl.BlockSpec(memory_space=pl.ANY), pl.BlockSpec(memory_space=pltpu.VMEM)),
        scratch_shapes=scratch,
        compiler_params=pltpu.CompilerParams(
            collective_id=0, has_side_effects=True, vmem_limit_bytes=40 * 1024 * 1024
        ),
        cost_estimate=pl.CostEstimate(flops=40_000_000, bytes_accessed=11_000_000, transcendentals=0),
    )(*[pltpu.with_memory_space_constraint(a, pltpu.HBM) for a in (block_columns, anchor_hour, trip_counts, dest_hour, daily_target)])
    return fitted, gap


def solution(mesh):
    placed = (
        P("tm", "orig", None, None),
        P("tm", "orig"),
        P("tm", None),
        P("orig", None, None),
        P("orig"),
    )
    return jax.shard_map(
        on_device,
        mesh=mesh,
        in_specs=placed,
        out_specs=(P("tm", "orig", None, None), P("tm", "orig")),
        check_vma=False,
    )
```

```python
import jax
import jax.numpy as jnp
from jax import lax
from jax.experimental import pallas as pl
from jax.experimental.pallas import tpu as pltpu
from jax.sharding import PartitionSpec as P

BINS = 3
SLOTS = 12
SIDE = 256
LANES = 128
CHIPS_Z, CHIPS_Y = 8, 4
CHIPS = CHIPS_Z * CHIPS_Y
OWN = 8
KEYS = 128
ROWS = 64
LAG = 2
F32 = jnp.float32


def hops(offset):
    return min(offset[0], CHIPS_Z - offset[0]) + min(offset[1], CHIPS_Y - offset[1])


OFFSETS = sorted(
    [(a, b) for a in range(CHIPS_Z) for b in range(CHIPS_Y) if (a, b) != (0, 0)], key=hops, reverse=True
)


def send(src, dst, send_sem, recv_sem, tm, orig):
    return pltpu.make_async_remote_copy(
        src_ref=src,
        dst_ref=dst,
        send_sem=send_sem,
        recv_sem=recv_sem,
        device_id=(tm, orig),
        device_id_type=pl.DeviceIdType.MESH,
    )


def kernel(
    cols_ref, anchor_ref, trips_ref, dest_ref, target_ref,
    fitted_ref, gap_ref,
    trips, part, factor, half_in, quarter_in, target, row_acc, anchor_fit, dest_row, dest8,
    onehot, sums, spread, gains, wide, wide_in, narrow, narrow_in,
    wide2, wide2_in, narrow2, narrow2_in,
    trips_sem, target_sem, dest_sem, fitted_sem,
    half_s, half_r, quarter_s, quarter_r, back_s, back_r, whole_s, whole_r,
    wide_sem, narrow_s, narrow_r, gain_sem, gain_s, gain_r, wide2_sem, narrow2_s, narrow2_r,
):
    x = lax.axis_index("tm")
    q = lax.axis_index("orig")
    chip, core = q // 2, q % 2
    z, y = chip // CHIPS_Y, chip % CHIPS_Y
    v = x // 2
    u = (x + v) % 2
    pa = x + 1 - 2 * (x % 2)
    pb = 3 - x
    other = chip * 2 + 1 - core
    chips = [((z + a) % CHIPS_Z) * CHIPS_Y + (y + b) % CHIPS_Y for a, b in OFFSETS]

    barrier = pltpu.get_barrier_semaphore()
    partners = [(x, 2 * o + core) for o in chips] + [(x, other), (pa, q), (pb, q)]
    for t_, o_ in partners:
        pl.semaphore_signal(barrier, inc=1, device_id=(t_, o_), device_id_type=pl.DeviceIdType.MESH)

    first, second = (pa, pb), (pb, pa)
    keep1, keep2 = (u, v), (v, u)
    kept64 = [pl.multiple_of(128 * h + 64 * keep1[h], 64) for h in range(2)]
    sent64 = [pl.multiple_of(128 * h + 64 * (1 - keep1[h]), 64) for h in range(2)]
    kept32 = [pl.multiple_of(kept64[h] + 32 * keep2[h], 32) for h in range(2)]
    sent32 = [pl.multiple_of(kept64[h] + 32 * (1 - keep2[h]), 32) for h in range(2)]

    def load_trips(s):
        return pltpu.make_async_copy(trips_ref.at[:, s], trips.at[s], trips_sem.at[s])

    def load_target(h):
        return pltpu.make_async_copy(
            target_ref.at[:, pl.ds(kept32[h], 32), :], target.at[h], target_sem.at[h]
        )

    load_dest = pltpu.make_async_copy(
        dest_ref.at[:, pl.ds(pl.multiple_of(q * 512, 512), 512)], dest_row, dest_sem
    )

    @pl.loop(0, SLOTS)
    def _(s):
        load_trips(s).start()

    load_dest.start()
    for h in range(2):
        load_target(h).start()

    r = lax.broadcasted_iota(jnp.int32, (2 * CHIPS * OWN, KEYS), 0)
    block = 4 * ((r >> 3) & (CHIPS - 1)) + 2 * (r >> 8) + (r & 1)
    row_key = jnp.where((r & 7) < 2 * BINS, block * BINS + ((r & 7) >> 1), -2)
    lane = lax.broadcasted_iota(jnp.int32, (1, KEYS), 1)
    key = jnp.full((1, KEYS), -1, jnp.int32)
    for s in range(SLOTS):
        col = cols_ref[s]
        in_slot = (lane >= 8 * s) & (lane < 8 * s + BINS) & (jnp.full((1, KEYS), col, jnp.int32) >= 0)
        key = jnp.where(in_slot, col * BINS + lane - 8 * s, key)
    onehot[...] = jnp.where(row_key == key, 1.0, 0.0).astype(F32).reshape(2, CHIPS * OWN, KEYS)

    diagonal = lax.broadcasted_iota(jnp.int32, (SIDE, SIDE), 0) == lax.broadcasted_iota(
        jnp.int32, (SIDE, SIDE), 1
    )
    row_acc[...] = jnp.zeros_like(row_acc)
    sums[...] = jnp.zeros_like(sums)
    dest8[...] = jnp.ones_like(dest8)

    @pl.loop(0, SLOTS)
    def _(s):
        load_trips(s).wait()
        live = jnp.where(cols_ref[s] >= 0, 1.0, 0.0).astype(F32)
        for t in range(BINS):
            for c in range(SIDE // ROWS):
                rows = pl.ds(c * ROWS, ROWS)
                left = trips[s, t, rows, pl.ds(0, LANES)].astype(F32)
                right = trips[s, t, rows, pl.ds(LANES, LANES)].astype(F32)
                row_acc[t, rows, :] += (left + right) * live

    for t in range(BINS):
        hour = jnp.sum(jnp.where(diagonal, anchor_ref[pl.ds(t, 1), :], 0.0), axis=1, keepdims=True)
        total = jnp.sum(row_acc[t], axis=1, keepdims=True)
        anchor_fit[t] = jnp.broadcast_to(hour / total, (SIDE, LANES))

    @pl.loop(0, SLOTS)
    def _(s):
        for t in range(BINS):
            for l in range(SIDE // LANES):
                lanes = pl.ds(l * LANES, LANES)
                acc = jnp.zeros((ROWS, LANES), F32)
                for c in range(SIDE // ROWS):
                    rows = pl.ds(c * ROWS, ROWS)
                    acc += trips[s, t, rows, lanes].astype(F32) * anchor_fit[t, rows, :]
                sums[s, pl.ds(t, 1), lanes] = jnp.sum(acc, axis=0, keepdims=True)

    pl.semaphore_wait(barrier, len(partners))

    def owner_sums(wide, wide_in, narrow, narrow_in, wide_sem, narrow_s, narrow_r):
        def by_owner(c):
            return jnp.dot(
                onehot[c], sums[...].reshape(KEYS, SIDE), precision=lax.Precision.HIGHEST, preferred_element_type=F32
            ).reshape(CHIPS, OWN, SIDE)

        wide[...] = by_owner(1 - core)
        copies = [send(wide, wide_in, wide_sem.at[0], wide_sem.at[1], x, other)]
        copies[0].start()
        kept = by_owner(core)
        copies[0].wait_recv()
        narrow[...] = kept + wide_in[...]
        for i, o in enumerate(chips):
            copies.append(send(narrow.at[o], narrow_in.at[i], narrow_s.at[i], narrow_r.at[i], x, 2 * o + core))
            copies[-1].start()
        total = narrow[chip]
        for i in reversed(range(len(chips))):
            copies[1 + i].wait_recv()
            total = total + narrow_in[i]
        return total, copies

    load_dest.wait()
    for t in range(BINS):
        for b in range(2):
            dest8[pl.ds(2 * t + b, 1), :] = dest_row[pl.ds(t, 1), pl.ds(b * SIDE, SIDE)]

    total, pending = owner_sums(wide, wide_in, narrow, narrow_in, wide_sem, narrow_s, narrow_r)
    gains[core, chip] = dest8[...] / jnp.maximum(total, 1.0)
    copies = []
    for i, o in enumerate(chips):
        mine = gains.at[core, chip]
        copies.append(send(mine, mine, gain_s.at[i], gain_r.at[i], x, 2 * o + core))
        copies[-1].start()
    for copy in copies:
        copy.wait_recv()
    swap = send(gains.at[core], gains.at[core], gain_sem.at[0], gain_sem.at[1], x, other)
    swap.start()

    def by_slot(c):
        return lax.dot_general(
            onehot[c], gains[c].reshape(CHIPS * OWN, SIDE), (((0,), (0,)), ((), ())),
            precision=lax.Precision.HIGHEST, preferred_element_type=F32,
        ).reshape(KEYS // 8, 8, SIDE)

    near = by_slot(core)
    swap.wait_recv()
    spread[...] = near + by_slot(1 - core)
    pending += copies + [swap]
    for h in range(2):
        load_target(h).wait()

    def halves(s, h):
        return send(
            part.at[s, pl.ds(sent64[h], 64), :], half_in.at[s, h], half_s.at[s, h], half_r.at[s, h], first[h], q
        )

    def quarters(s, h):
        return send(
            part.at[s, pl.ds(sent32[h], 32), :], quarter_in.at[s, h], quarter_s.at[s, h], quarter_r.at[s, h], second[h], q
        )

    def back(s, h):
        rows = pl.ds(kept32[h], 32)
        return send(factor.at[s, rows, :], factor.at[s, rows, :], back_s.at[s, h], back_r.at[s, h], second[h], q)

    def whole(s, h):
        rows = pl.ds(kept64[h], 64)
        return send(factor.at[s, rows, :], factor.at[s, rows, :], whole_s.at[s, h], whole_r.at[s, h], first[h], q)

    def store_fitted(s):
        return pltpu.make_async_copy(trips.at[s], fitted_ref.at[:, s], fitted_sem.at[s])

    @pl.loop(0, SLOTS + 4 * LAG)
    def _(k):
        @pl.when(k < SLOTS)
        def _():
            s = k
            for l in range(SIDE // LANES):
                lanes = pl.ds(l * LANES, LANES)
                gain = [spread[s, pl.ds(t, 1), lanes] for t in range(BINS)]
                for c in range(SIDE // ROWS):
                    rows = pl.ds(c * ROWS, ROWS)
                    acc = jnp.zeros((ROWS, LANES), F32)
                    for t in range(BINS):
                        acc += trips[s, t, rows, lanes].astype(F32) * anchor_fit[t, rows, :] * gain[t]
                    part[s, rows, lanes] = acc
            for h in range(2):
                halves(s, h).start()

        @pl.when((k >= LAG) & (k < SLOTS + LAG))
        def _():
            s = k - LAG
            for h in range(2):
                halves(s, h).wait_recv()
                part[s, pl.ds(kept64[h], 64), :] += half_in[s, h]
                quarters(s, h).start()

        @pl.when((k >= 2 * LAG) & (k < SLOTS + 2 * LAG))
        def _():
            s = k - 2 * LAG
            dead = jnp.where(cols_ref[s] >= 0, 0.0, 1.0).astype(F32)
            for h in range(2):
                quarters(s, h).wait_recv()
                rows = pl.ds(kept32[h], 32)
                daily = part[s, rows, :] + quarter_in[s, h]
                factor[s, rows, :] = target[h, s].astype(F32) / (daily + dead)
                back(s, h).start()

        @pl.when((k >= 3 * LAG) & (k < SLOTS + 3 * LAG))
        def _():
            s = k - 3 * LAG
            for h in range(2):
                back(s, h).wait_recv()
                whole(s, h).start()

        @pl.when(k >= 4 * LAG)
        def _():
            s = k - 4 * LAG
            for h in range(2):
                whole(s, h).wait_recv()
            for t in range(BINS):
                for l in range(SIDE // LANES):
                    lanes = pl.ds(l * LANES, LANES)
                    gain = spread[s, pl.ds(t, 1), lanes]
                    acc = jnp.zeros((ROWS, LANES), F32)
                    for c in range(SIDE // ROWS):
                        rows = pl.ds(c * ROWS, ROWS)
                        value = trips[s, t, rows, lanes].astype(F32) * anchor_fit[t, rows, :] * factor[s, rows, lanes]
                        acc += value
                        trips[s, t, rows, lanes] = (value * gain).astype(jnp.bfloat16)
                    sums[s, pl.ds(t, 1), lanes] = jnp.sum(acc, axis=0, keepdims=True) * gain
            store_fitted(s).start()

    total, more = owner_sums(wide2, wide2_in, narrow2, narrow2_in, wide2_sem, narrow2_s, narrow2_r)
    pending += more
    gap = total / dest8[...] - 1.0
    for t in range(BINS):
        for b in range(2):
            gap_ref[pl.ds(t, 1), pl.ds(b * SIDE, SIDE)] = gap[2 * t + b : 2 * t + b + 1, :]

    for copy in pending:
        copy.wait_send()

    @pl.loop(0, SLOTS)
    def _(s):
        for h in range(2):
            halves(s, h).wait_send()
            quarters(s, h).wait_send()
            back(s, h).wait_send()
            whole(s, h).wait_send()
        store_fitted(s).wait()


def on_device(trip_counts, anchor_hour, dest_hour, daily_target, block_columns):
    vmem = lambda *shape: pltpu.VMEM(shape, F32)
    dma = lambda *shape: pltpu.SemaphoreType.DMA(shape)
    scratch = [
        pltpu.VMEM((SLOTS, BINS, SIDE, SIDE), jnp.bfloat16),
        vmem(SLOTS, SIDE, SIDE),
        vmem(SLOTS, SIDE, SIDE),
        vmem(SLOTS, 2, 64, SIDE),
        vmem(SLOTS, 2, 32, SIDE),
        pltpu.VMEM((2, SLOTS, 32, SIDE), jnp.bfloat16),
        vmem(BINS, SIDE, LANES),
        vmem(BINS, SIDE, LANES),
        vmem(BINS, 512),
        vmem(8, SIDE),
        vmem(2, CHIPS * OWN, KEYS),
        vmem(KEYS // 8, 8, SIDE),
        vmem(KEYS // 8, 8, SIDE),
        vmem(2, CHIPS, OWN, SIDE),
    ] + [vmem(CHIPS, OWN, SIDE), vmem(CHIPS, OWN, SIDE), vmem(CHIPS, OWN, SIDE), vmem(CHIPS - 1, OWN, SIDE)] * 2 + [
        dma(SLOTS), dma(2), pltpu.SemaphoreType.DMA, dma(SLOTS),
    ] + [dma(SLOTS, 2)] * 8 + [dma(2), dma(CHIPS - 1), dma(CHIPS - 1)] * 3
    fitted, gap = pl.pallas_call(
        kernel,
        out_shape=(
            jax.ShapeDtypeStruct(trip_counts.shape, jnp.bfloat16),
            jax.ShapeDtypeStruct((BINS, 512), F32),
        ),
        in_specs=[
            pl.BlockSpec(memory_space=pltpu.SMEM),
            pl.BlockSpec(memory_space=pltpu.VMEM),
            pl.BlockSpec(memory_space=pl.ANY),
            pl.BlockSpec(memory_space=pl.ANY),
            pl.BlockSpec(memory_space=pl.ANY),
        ],
        out_specs=(pl.BlockSpec(memory_space=pl.ANY), pl.BlockSpec(memory_space=pltpu.VMEM)),
        scratch_shapes=scratch,
        compiler_params=pltpu.CompilerParams(
            collective_id=0, has_side_effects=True, vmem_limit_bytes=40 * 1024 * 1024
        ),
        cost_estimate=pl.CostEstimate(flops=40_000_000, bytes_accessed=11_000_000, transcendentals=0),
    )(*[pltpu.with_memory_space_constraint(a, pltpu.HBM) for a in (block_columns, anchor_hour, trip_counts, dest_hour, daily_target)])
    return fitted, gap


def solution(mesh):
    placed = (
        P("tm", "orig", None, None),
        P("tm", "orig"),
        P("tm", None),
        P("orig", None, None),
        P("orig"),
    )
    return jax.shard_map(
        on_device,
        mesh=mesh,
        in_specs=placed,
        out_specs=(P("tm", "orig", None, None), P("tm", "orig")),
        check_vma=False,
    )
```

```python
import jax
import jax.numpy as jnp
from jax import lax
from jax.experimental import pallas as pl
from jax.experimental.pallas import tpu as pltpu
from jax.sharding import PartitionSpec as P

BINS = 3
SLOTS = 12
SIDE = 256
LANES = 128
CHIPS_Z, CHIPS_Y = 8, 4
CHIPS = CHIPS_Z * CHIPS_Y
OWN = 8
KEYS = 128
ROWS = 64
EARLY = 4
LAG = 2
F32 = jnp.float32


def hops(offset):
    return min(offset[0], CHIPS_Z - offset[0]) + min(offset[1], CHIPS_Y - offset[1])


OFFSETS = sorted(
    [(a, b) for a in range(CHIPS_Z) for b in range(CHIPS_Y) if (a, b) != (0, 0)], key=hops, reverse=True
)


def send(src, dst, send_sem, recv_sem, tm, orig):
    return pltpu.make_async_remote_copy(
        src_ref=src,
        dst_ref=dst,
        send_sem=send_sem,
        recv_sem=recv_sem,
        device_id=(tm, orig),
        device_id_type=pl.DeviceIdType.MESH,
    )


def kernel(
    cols_ref, anchor_ref, trips_ref, dest_ref, target_ref,
    fitted_ref, gap_ref,
    trips, part, factor, half_in, quarter_in, target, row_acc, anchor_fit, dest_row, dest8,
    onehot, sums, spread, gains, wide, wide_in, narrow, narrow_in,
    wide2, wide2_in, narrow2, narrow2_in, ship, ship_in, peer,
    trips_sem, target_sem, dest_sem, fitted_sem,
    half_s, half_r, quarter_s, quarter_r, back_s, back_r, whole_s, whole_r,
    wide_sem, narrow_s, narrow_r, gain_sem, gain_s, gain_r, wide2_sem, narrow2_s, narrow2_r,
    ship_s, ship_r, peer_s, peer_r,
):
    x = lax.axis_index("tm")
    q = lax.axis_index("orig")
    chip, core = q // 2, q % 2
    z, y = chip // CHIPS_Y, chip % CHIPS_Y
    v = x // 2
    u = (x + v) % 2
    pa = x + 1 - 2 * (x % 2)
    pb = 3 - x
    other = chip * 2 + 1 - core
    chips = [((z + a) % CHIPS_Z) * CHIPS_Y + (y + b) % CHIPS_Y for a, b in OFFSETS]

    barrier = pltpu.get_barrier_semaphore()
    partners = [(x, 2 * o + core) for o in chips] + [(x, other), (pa, q), (pb, q)]
    for t_, o_ in partners:
        pl.semaphore_signal(barrier, inc=1, device_id=(t_, o_), device_id_type=pl.DeviceIdType.MESH)

    first, second = (pa, pb), (pb, pa)
    keep1, keep2 = (u, v), (v, u)
    kept64 = [pl.multiple_of(128 * h + 64 * keep1[h], 64) for h in range(2)]
    sent64 = [pl.multiple_of(128 * h + 64 * (1 - keep1[h]), 64) for h in range(2)]
    kept32 = [pl.multiple_of(kept64[h] + 32 * keep2[h], 32) for h in range(2)]
    sent32 = [pl.multiple_of(kept64[h] + 32 * (1 - keep2[h]), 32) for h in range(2)]

    def load_trips(s):
        return pltpu.make_async_copy(trips_ref.at[:, s], trips.at[s], trips_sem.at[s])

    def load_target(h):
        return pltpu.make_async_copy(
            target_ref.at[:, pl.ds(kept32[h], 32), :], target.at[h], target_sem.at[h]
        )

    load_dest = pltpu.make_async_copy(
        dest_ref.at[:, pl.ds(pl.multiple_of(q * 512, 512), 512)], dest_row, dest_sem
    )

    @pl.loop(0, SLOTS)
    def _(s):
        load_trips(s).start()

    load_dest.start()
    for h in range(2):
        load_target(h).start()

    r = lax.broadcasted_iota(jnp.int32, (2 * CHIPS * OWN, KEYS), 0)
    block = 4 * ((r >> 3) & (CHIPS - 1)) + 2 * (r >> 8) + (r & 1)
    row_key = jnp.where((r & 7) < 2 * BINS, block * BINS + ((r & 7) >> 1), -2)
    lane = lax.broadcasted_iota(jnp.int32, (1, KEYS), 1)
    key = jnp.full((1, KEYS), -1, jnp.int32)
    for s in range(SLOTS):
        col = cols_ref[s]
        in_slot = (lane >= 8 * s) & (lane < 8 * s + BINS) & (jnp.full((1, KEYS), col, jnp.int32) >= 0)
        key = jnp.where(in_slot, col * BINS + lane - 8 * s, key)
    onehot[...] = jnp.where(row_key == key, 1.0, 0.0).astype(F32).reshape(2, CHIPS * OWN, KEYS)

    diagonal = lax.broadcasted_iota(jnp.int32, (SIDE, SIDE), 0) == lax.broadcasted_iota(
        jnp.int32, (SIDE, SIDE), 1
    )
    row_acc[...] = jnp.zeros_like(row_acc)
    sums[...] = jnp.zeros_like(sums)
    dest8[...] = jnp.ones_like(dest8)

    @pl.loop(0, SLOTS)
    def _(s):
        load_trips(s).wait()
        live = jnp.where(cols_ref[s] >= 0, 1.0, 0.0).astype(F32)
        for t in range(BINS):
            for c in range(SIDE // ROWS):
                rows = pl.ds(c * ROWS, ROWS)
                left = trips[s, t, rows, pl.ds(0, LANES)].astype(F32)
                right = trips[s, t, rows, pl.ds(LANES, LANES)].astype(F32)
                row_acc[t, rows, :] += (left + right) * live

    for t in range(BINS):
        hour = jnp.sum(jnp.where(diagonal, anchor_ref[pl.ds(t, 1), :], 0.0), axis=1, keepdims=True)
        total = jnp.sum(row_acc[t], axis=1, keepdims=True)
        anchor_fit[t] = jnp.broadcast_to(hour / total, (SIDE, LANES))

    @pl.loop(0, SLOTS)
    def _(s):
        for t in range(BINS):
            for l in range(SIDE // LANES):
                lanes = pl.ds(l * LANES, LANES)
                acc = jnp.zeros((ROWS, LANES), F32)
                for c in range(SIDE // ROWS):
                    rows = pl.ds(c * ROWS, ROWS)
                    acc += trips[s, t, rows, lanes].astype(F32) * anchor_fit[t, rows, :]
                sums[s, pl.ds(t, 1), lanes] = jnp.sum(acc, axis=0, keepdims=True)

    pl.semaphore_wait(barrier, len(partners))

    def owner_sums(wide, wide_in, narrow, narrow_in, wide_sem, narrow_s, narrow_r, meanwhile):
        def by_owner(c):
            return jnp.dot(
                onehot[c], sums[...].reshape(KEYS, SIDE), precision=lax.Precision.HIGHEST, preferred_element_type=F32
            ).reshape(CHIPS, OWN, SIDE)

        wide[...] = by_owner(1 - core)
        copies = [send(wide, wide_in, wide_sem.at[0], wide_sem.at[1], x, other)]
        copies[0].start()
        kept = by_owner(core)
        copies[0].wait_recv()
        narrow[...] = kept + wide_in[...]
        for i, o in enumerate(chips):
            copies.append(send(narrow.at[o], narrow_in.at[i], narrow_s.at[i], narrow_r.at[i], x, 2 * o + core))
            copies[-1].start()
        meanwhile()
        total = narrow[chip]
        for i in reversed(range(len(chips))):
            copies[1 + i].wait_recv()
            total = total + narrow_in[i]
        return total, copies

    def shipped(s, h):
        return send(ship.at[s, h], ship_in.at[s, h], ship_s.at[s, h], ship_r.at[s, h], first[h], q)

    def ship_early():
        @pl.loop(0, EARLY)
        def _(s):
            for h in range(2):
                rows = pl.ds(sent64[h], 64)
                for t in range(BINS):
                    for l in range(SIDE // LANES):
                        lanes = pl.ds(l * LANES, LANES)
                        ship[s, h, t, :, lanes] = trips[s, t, rows, lanes].astype(F32) * anchor_fit[t, rows, :]
                shipped(s, h).start()

    load_dest.wait()
    for t in range(BINS):
        for b in range(2):
            dest8[pl.ds(2 * t + b, 1), :] = dest_row[pl.ds(t, 1), pl.ds(b * SIDE, SIDE)]

    total, pending = owner_sums(wide, wide_in, narrow, narrow_in, wide_sem, narrow_s, narrow_r, ship_early)
    gains[core, chip] = dest8[...] / jnp.maximum(total, 1.0)
    copies = []
    for i, o in enumerate(chips):
        mine = gains.at[core, chip]
        copies.append(send(mine, mine, gain_s.at[i], gain_r.at[i], x, 2 * o + core))
        copies[-1].start()
    for copy in copies:
        copy.wait_recv()
    swap = send(gains.at[core], gains.at[core], gain_sem.at[0], gain_sem.at[1], x, other)
    swap.start()

    def by_slot(c):
        return lax.dot_general(
            onehot[c], gains[c].reshape(CHIPS * OWN, SIDE), (((0,), (0,)), ((), ())),
            precision=lax.Precision.HIGHEST, preferred_element_type=F32,
        ).reshape(KEYS // 8, 8, SIDE)

    near = by_slot(core)
    swap.wait_recv()
    spread[...] = near + by_slot(1 - core)
    pending += copies + [swap]
    early_slots = pl.ds(0, EARLY)
    swaps = [
        send(spread.at[early_slots], peer.at[h], peer_s.at[h], peer_r.at[h], first[h], q) for h in range(2)
    ]
    for copy in swaps:
        copy.start()
    pending += swaps
    for h in range(2):
        load_target(h).wait()

    def halves(s, h):
        return send(
            part.at[s, pl.ds(sent64[h], 64), :], half_in.at[s, h], half_s.at[s, h], half_r.at[s, h], first[h], q
        )

    def quarters(s, h):
        return send(
            part.at[s, pl.ds(sent32[h], 32), :], quarter_in.at[s, h], quarter_s.at[s, h], quarter_r.at[s, h], second[h], q
        )

    def back(s, h):
        rows = pl.ds(kept32[h], 32)
        return send(factor.at[s, rows, :], factor.at[s, rows, :], back_s.at[s, h], back_r.at[s, h], second[h], q)

    def whole(s, h):
        rows = pl.ds(kept64[h], 64)
        return send(factor.at[s, rows, :], factor.at[s, rows, :], whole_s.at[s, h], whole_r.at[s, h], first[h], q)

    def store_fitted(s):
        return pltpu.make_async_copy(trips.at[s], fitted_ref.at[:, s], fitted_sem.at[s])

    @pl.loop(0, SLOTS + 4 * LAG)
    def _(k):
        @pl.when(k < SLOTS - EARLY)
        def _():
            s = k + EARLY
            for l in range(SIDE // LANES):
                lanes = pl.ds(l * LANES, LANES)
                gain = [spread[s, pl.ds(t, 1), lanes] for t in range(BINS)]
                for c in range(SIDE // ROWS):
                    rows = pl.ds(c * ROWS, ROWS)
                    acc = jnp.zeros((ROWS, LANES), F32)
                    for t in range(BINS):
                        acc += trips[s, t, rows, lanes].astype(F32) * anchor_fit[t, rows, :] * gain[t]
                    part[s, rows, lanes] = acc
            for h in range(2):
                halves(s, h).start()

        @pl.when(k == SLOTS - EARLY + LAG)
        def _():
            for copy in swaps:
                copy.wait_recv()

        @pl.when((k >= SLOTS - EARLY + LAG) & (k < SLOTS + LAG))
        def _():
            s = k - LAG - (SLOTS - EARLY)
            for h in range(2):
                shipped(s, h).wait_recv()
                rows = pl.ds(kept64[h], 64)
                for l in range(SIDE // LANES):
                    lanes = pl.ds(l * LANES, LANES)
                    acc = jnp.zeros((64, LANES), F32)
                    for t in range(BINS):
                        fit = trips[s, t, rows, lanes].astype(F32) * anchor_fit[t, rows, :]
                        acc += fit * spread[s, pl.ds(t, 1), lanes]
                        acc += ship_in[s, h, t, :, lanes] * peer[h, s, pl.ds(t, 1), lanes]
                    part[s, rows, lanes] = acc
                quarters(s, h).start()

        @pl.when((k >= LAG) & (k < SLOTS - EARLY + LAG))
        def _():
            s = k - LAG + EARLY
            for h in range(2):
                halves(s, h).wait_recv()
                part[s, pl.ds(kept64[h], 64), :] += half_in[s, h]
                quarters(s, h).start()

        @pl.when((k >= 2 * LAG) & (k < SLOTS + 2 * LAG))
        def _():
            s = lax.rem(k - 2 * LAG + EARLY, SLOTS)
            dead = jnp.where(cols_ref[s] >= 0, 0.0, 1.0).astype(F32)
            for h in range(2):
                quarters(s, h).wait_recv()
                rows = pl.ds(kept32[h], 32)
                daily = part[s, rows, :] + quarter_in[s, h]
                factor[s, rows, :] = target[h, s].astype(F32) / (daily + dead)
                back(s, h).start()

        @pl.when((k >= 3 * LAG) & (k < SLOTS + 3 * LAG))
        def _():
            s = lax.rem(k - 3 * LAG + EARLY, SLOTS)
            for h in range(2):
                back(s, h).wait_recv()
                whole(s, h).start()

        @pl.when(k >= 4 * LAG)
        def _():
            s = lax.rem(k - 4 * LAG + EARLY, SLOTS)
            for h in range(2):
                whole(s, h).wait_recv()
            for t in range(BINS):
                for l in range(SIDE // LANES):
                    lanes = pl.ds(l * LANES, LANES)
                    gain = spread[s, pl.ds(t, 1), lanes]
                    acc = jnp.zeros((ROWS, LANES), F32)
                    for c in range(SIDE // ROWS):
                        rows = pl.ds(c * ROWS, ROWS)
                        value = trips[s, t, rows, lanes].astype(F32) * anchor_fit[t, rows, :] * factor[s, rows, lanes]
                        acc += value
                        trips[s, t, rows, lanes] = (value * gain).astype(jnp.bfloat16)
                    sums[s, pl.ds(t, 1), lanes] = jnp.sum(acc, axis=0, keepdims=True) * gain
            store_fitted(s).start()

    total, more = owner_sums(wide2, wide2_in, narrow2, narrow2_in, wide2_sem, narrow2_s, narrow2_r, lambda: None)
    pending += more
    gap = total / dest8[...] - 1.0
    for t in range(BINS):
        for b in range(2):
            gap_ref[pl.ds(t, 1), pl.ds(b * SIDE, SIDE)] = gap[2 * t + b : 2 * t + b + 1, :]

    for copy in pending:
        copy.wait_send()

    @pl.loop(0, EARLY)
    def _(s):
        for h in range(2):
            shipped(s, h).wait_send()

    @pl.loop(EARLY, SLOTS)
    def _(s):
        for h in range(2):
            halves(s, h).wait_send()

    @pl.loop(0, SLOTS)
    def _(s):
        for h in range(2):
            quarters(s, h).wait_send()
            back(s, h).wait_send()
            whole(s, h).wait_send()
        store_fitted(s).wait()


def on_device(trip_counts, anchor_hour, dest_hour, daily_target, block_columns):
    vmem = lambda *shape: pltpu.VMEM(shape, F32)
    dma = lambda *shape: pltpu.SemaphoreType.DMA(shape)
    scratch = [
        pltpu.VMEM((SLOTS, BINS, SIDE, SIDE), jnp.bfloat16),
        vmem(SLOTS, SIDE, SIDE),
        vmem(SLOTS, SIDE, SIDE),
        vmem(SLOTS, 2, 64, SIDE),
        vmem(SLOTS, 2, 32, SIDE),
        pltpu.VMEM((2, SLOTS, 32, SIDE), jnp.bfloat16),
        vmem(BINS, SIDE, LANES),
        vmem(BINS, SIDE, LANES),
        vmem(BINS, 512),
        vmem(8, SIDE),
        vmem(2, CHIPS * OWN, KEYS),
        vmem(KEYS // 8, 8, SIDE),
        vmem(KEYS // 8, 8, SIDE),
        vmem(2, CHIPS, OWN, SIDE),
    ] + [vmem(CHIPS, OWN, SIDE), vmem(CHIPS, OWN, SIDE), vmem(CHIPS, OWN, SIDE), vmem(CHIPS - 1, OWN, SIDE)] * 2 + [
        vmem(EARLY, 2, BINS, 64, SIDE),
        vmem(EARLY, 2, BINS, 64, SIDE),
        vmem(2, EARLY, 8, SIDE),
        dma(SLOTS), dma(2), pltpu.SemaphoreType.DMA, dma(SLOTS),
    ] + [dma(SLOTS, 2)] * 8 + [dma(2), dma(CHIPS - 1), dma(CHIPS - 1)] * 3 + [dma(EARLY, 2)] * 2 + [dma(2)] * 2
    fitted, gap = pl.pallas_call(
        kernel,
        out_shape=(
            jax.ShapeDtypeStruct(trip_counts.shape, jnp.bfloat16),
            jax.ShapeDtypeStruct((BINS, 512), F32),
        ),
        in_specs=[
            pl.BlockSpec(memory_space=pltpu.SMEM),
            pl.BlockSpec(memory_space=pltpu.VMEM),
            pl.BlockSpec(memory_space=pl.ANY),
            pl.BlockSpec(memory_space=pl.ANY),
            pl.BlockSpec(memory_space=pl.ANY),
        ],
        out_specs=(pl.BlockSpec(memory_space=pl.ANY), pl.BlockSpec(memory_space=pltpu.VMEM)),
        scratch_shapes=scratch,
        compiler_params=pltpu.CompilerParams(
            collective_id=0, has_side_effects=True, vmem_limit_bytes=40 * 1024 * 1024
        ),
        cost_estimate=pl.CostEstimate(flops=40_000_000, bytes_accessed=11_000_000, transcendentals=0),
    )(*[pltpu.with_memory_space_constraint(a, pltpu.HBM) for a in (block_columns, anchor_hour, trip_counts, dest_hour, daily_target)])
    return fitted, gap


def solution(mesh):
    placed = (
        P("tm", "orig", None, None),
        P("tm", "orig"),
        P("tm", None),
        P("orig", None, None),
        P("orig"),
    )
    return jax.shard_map(
        on_device,
        mesh=mesh,
        in_specs=placed,
        out_specs=(P("tm", "orig", None, None), P("tm", "orig")),
        check_vma=False,
    )
```

```python
import jax
import jax.numpy as jnp
from jax import lax
from jax.experimental import pallas as pl
from jax.experimental.pallas import tpu as pltpu
from jax.sharding import PartitionSpec as P

BINS = 3
SLOTS = 12
SIDE = 256
LANES = 128
CHIPS_Z, CHIPS_Y = 8, 4
CHIPS = CHIPS_Z * CHIPS_Y
OWN = 8
USED = 2 * BINS
KEYS = 128
ROWS = 64
EARLY = 4
AT_ONCE = 1
LAG = 2
F32 = jnp.float32
BF16 = jnp.bfloat16


def picked(onehot, values):
    high = values.astype(BF16)
    rest = values - high.astype(F32)
    middle = rest.astype(BF16)
    low = (rest - middle.astype(F32)).astype(BF16)
    return sum(jnp.dot(onehot, part, preferred_element_type=F32) for part in (low, middle, high))


def hops(offset):
    return min(offset[0], CHIPS_Z - offset[0]) + min(offset[1], CHIPS_Y - offset[1])


OFFSETS = sorted(
    [(a, b) for a in range(CHIPS_Z) for b in range(CHIPS_Y) if (a, b) != (0, 0)], key=hops, reverse=True
)


def send(src, dst, send_sem, recv_sem, tm, orig):
    return pltpu.make_async_remote_copy(
        src_ref=src,
        dst_ref=dst,
        send_sem=send_sem,
        recv_sem=recv_sem,
        device_id=(tm, orig),
        device_id_type=pl.DeviceIdType.MESH,
    )


def kernel(
    cols_ref, anchor_ref, trips_ref, dest_ref, target_ref,
    fitted_ref, gap_ref,
    trips, part, factor, half_in, quarter_in, target, row_acc, anchor_fit, dest_row, dest8,
    onehot, by_key, sums, spread, gains, wide, wide_in, narrow, narrow_in,
    wide2, wide2_in, narrow2, narrow2_in, ship, ship_in, peer,
    trips_sem, target_sem, dest_sem, fitted_sem,
    half_s, half_r, quarter_s, quarter_r, back_s, back_r, whole_s, whole_r,
    wide_sem, narrow_s, narrow_r, gain_sem, gain_s, gain_r, wide2_sem, narrow2_s, narrow2_r,
    ship_s, ship_r, peer_s, peer_r,
):
    x = lax.axis_index("tm")
    q = lax.axis_index("orig")
    chip, core = q // 2, q % 2
    z, y = chip // CHIPS_Y, chip % CHIPS_Y
    v = x // 2
    u = (x + v) % 2
    pa = x + 1 - 2 * (x % 2)
    pb = 3 - x
    other = chip * 2 + 1 - core
    chips = [((z + a) % CHIPS_Z) * CHIPS_Y + (y + b) % CHIPS_Y for a, b in OFFSETS]

    barrier = pltpu.get_barrier_semaphore()
    partners = [(x, 2 * o + core) for o in chips] + [(x, other), (pa, q), (pb, q)]
    for t_, o_ in partners:
        pl.semaphore_signal(barrier, inc=1, device_id=(t_, o_), device_id_type=pl.DeviceIdType.MESH)

    first, second = (pa, pb), (pb, pa)
    keep1, keep2 = (u, v), (v, u)
    kept64 = [pl.multiple_of(128 * h + 64 * keep1[h], 64) for h in range(2)]
    sent64 = [pl.multiple_of(128 * h + 64 * (1 - keep1[h]), 64) for h in range(2)]
    kept32 = [pl.multiple_of(kept64[h] + 32 * keep2[h], 32) for h in range(2)]
    sent32 = [pl.multiple_of(kept64[h] + 32 * (1 - keep2[h]), 32) for h in range(2)]

    def load_trips(s):
        return pltpu.make_async_copy(trips_ref.at[:, s], trips.at[s], trips_sem.at[s])

    def load_target(h):
        return pltpu.make_async_copy(
            target_ref.at[:, pl.ds(kept32[h], 32), :], target.at[h], target_sem.at[h]
        )

    load_dest = pltpu.make_async_copy(
        dest_ref.at[:, pl.ds(pl.multiple_of(q * 512, 512), 512)], dest_row, dest_sem
    )

    @pl.loop(0, SLOTS)
    def _(s):
        load_trips(s).start()

    load_dest.start()
    for h in range(2):
        load_target(h).start()

    r = lax.broadcasted_iota(jnp.int32, (2 * CHIPS * OWN, KEYS), 0)
    block = 4 * ((r >> 3) & (CHIPS - 1)) + 2 * (r >> 8) + (r & 1)
    row_key = jnp.where((r & 7) < 2 * BINS, block * BINS + ((r & 7) >> 1), -2)
    lane = lax.broadcasted_iota(jnp.int32, (1, KEYS), 1)
    key = jnp.full((1, KEYS), -1, jnp.int32)
    for s in range(SLOTS):
        col = cols_ref[s]
        in_slot = (lane >= 8 * s) & (lane < 8 * s + BINS) & (jnp.full((1, KEYS), col, jnp.int32) >= 0)
        key = jnp.where(in_slot, col * BINS + lane - 8 * s, key)
    match = jnp.where(row_key == key, 1.0, 0.0).astype(F32)
    for c in range(2):
        half = match[c * CHIPS * OWN : (c + 1) * CHIPS * OWN, :]
        onehot[c] = half.astype(BF16)
        by_key[c] = half.T.astype(BF16)

    diagonal = lax.broadcasted_iota(jnp.int32, (SIDE, SIDE), 0) == lax.broadcasted_iota(
        jnp.int32, (SIDE, SIDE), 1
    )
    row_acc[...] = jnp.zeros_like(row_acc)
    sums[...] = jnp.zeros_like(sums)
    gains[...] = jnp.zeros_like(gains)
    dest8[...] = jnp.ones_like(dest8)

    @pl.loop(0, SLOTS)
    def _(s):
        load_trips(s).wait()
        live = jnp.where(cols_ref[s] >= 0, 1.0, 0.0).astype(F32)
        for t in range(BINS):
            for c in range(SIDE // ROWS):
                rows = pl.ds(c * ROWS, ROWS)
                left = trips[s, t, rows, pl.ds(0, LANES)].astype(F32)
                right = trips[s, t, rows, pl.ds(LANES, LANES)].astype(F32)
                row_acc[t, rows, :] += (left + right) * live

    for t in range(BINS):
        hour = jnp.sum(jnp.where(diagonal, anchor_ref[pl.ds(t, 1), :], 0.0), axis=1, keepdims=True)
        total = jnp.sum(row_acc[t], axis=1, keepdims=True)
        anchor_fit[t] = jnp.broadcast_to(hour / total, (SIDE, LANES))

    @pl.loop(0, SLOTS)
    def _(s):
        for t in range(BINS):
            for l in range(SIDE // LANES):
                lanes = pl.ds(l * LANES, LANES)
                acc = jnp.zeros((ROWS, LANES), F32)
                for c in range(SIDE // ROWS):
                    rows = pl.ds(c * ROWS, ROWS)
                    acc += trips[s, t, rows, lanes].astype(F32) * anchor_fit[t, rows, :]
                sums[s, pl.ds(t, 1), lanes] = jnp.sum(acc, axis=0, keepdims=True)

    def shipped(s, h):
        return send(ship.at[s, h], ship_in.at[s, h], ship_s.at[s, h], ship_r.at[s, h], first[h], q)

    def fill_early(s):
        for h in range(2):
            rows = pl.ds(sent64[h], 64)
            for t in range(BINS):
                for l in range(SIDE // LANES):
                    lanes = pl.ds(l * LANES, LANES)
                    ship[s, h, t, :, lanes] = trips[s, t, rows, lanes].astype(F32) * anchor_fit[t, rows, :]

    def send_early(s):
        for h in range(2):
            shipped(s, h).start()

    def later_early():
        @pl.loop(AT_ONCE, EARLY)
        def _(s):
            fill_early(s)
            send_early(s)

    pl.loop(0, AT_ONCE)(fill_early)
    pl.semaphore_wait(barrier, len(partners))
    pl.loop(0, AT_ONCE)(send_early)

    used = pl.ds(0, USED)

    def owner_sums(wide, wide_in, narrow, narrow_in, wide_sem, narrow_s, narrow_r, meanwhile):
        def by_owner(c):
            return picked(onehot[c], sums[...].reshape(KEYS, SIDE)).reshape(CHIPS, OWN, SIDE)

        wide[...] = by_owner(1 - core)
        copies = [send(wide, wide_in, wide_sem.at[0], wide_sem.at[1], x, other)]
        copies[0].start()
        kept = by_owner(core)
        copies[0].wait_recv()
        narrow[...] = kept + wide_in[...]
        for i, o in enumerate(chips):
            copies.append(send(narrow.at[o, used, :], narrow_in.at[i, used, :], narrow_s.at[i], narrow_r.at[i], x, 2 * o + core))
            copies[-1].start()
        meanwhile()
        total = narrow[chip, used, :]
        for i in reversed(range(len(chips))):
            copies[1 + i].wait_recv()
            total = total + narrow_in[i, used, :]
        return total, copies

    load_dest.wait()
    for t in range(BINS):
        for b in range(2):
            dest8[pl.ds(2 * t + b, 1), :] = dest_row[pl.ds(t, 1), pl.ds(b * SIDE, SIDE)]

    total, pending = owner_sums(wide, wide_in, narrow, narrow_in, wide_sem, narrow_s, narrow_r, later_early)
    gains[core, chip, used, :] = dest8[used, :] / jnp.maximum(total, 1.0)
    copies = []
    for i, o in enumerate(chips):
        mine = gains.at[core, chip, used, :]
        copies.append(send(mine, mine, gain_s.at[i], gain_r.at[i], x, 2 * o + core))
        copies[-1].start()
    for copy in copies:
        copy.wait_recv()
    swap = send(gains.at[core], gains.at[core], gain_sem.at[0], gain_sem.at[1], x, other)
    swap.start()

    def by_slot(c):
        return picked(by_key[c], gains[c].reshape(CHIPS * OWN, SIDE)).reshape(KEYS // 8, 8, SIDE)

    near = by_slot(core)
    swap.wait_recv()
    spread[...] = near + by_slot(1 - core)
    pending += copies + [swap]
    early_slots = pl.ds(0, EARLY)
    swaps = [
        send(spread.at[early_slots], peer.at[h], peer_s.at[h], peer_r.at[h], first[h], q) for h in range(2)
    ]
    for copy in swaps:
        copy.start()
    pending += swaps
    for h in range(2):
        load_target(h).wait()

    def halves(s, h):
        return send(
            part.at[s, pl.ds(sent64[h], 64), :], half_in.at[s, h], half_s.at[s, h], half_r.at[s, h], first[h], q
        )

    def quarters(s, h):
        return send(
            part.at[s, pl.ds(sent32[h], 32), :], quarter_in.at[s, h], quarter_s.at[s, h], quarter_r.at[s, h], second[h], q
        )

    def back(s, h):
        rows = pl.ds(kept32[h], 32)
        return send(factor.at[s, rows, :], factor.at[s, rows, :], back_s.at[s, h], back_r.at[s, h], second[h], q)

    def whole(s, h):
        rows = pl.ds(kept64[h], 64)
        return send(factor.at[s, rows, :], factor.at[s, rows, :], whole_s.at[s, h], whole_r.at[s, h], first[h], q)

    def store_fitted(s):
        return pltpu.make_async_copy(trips.at[s], fitted_ref.at[:, s], fitted_sem.at[s])

    @pl.loop(0, SLOTS + 4 * LAG)
    def _(k):
        @pl.when(k < SLOTS - EARLY)
        def _():
            s = k + EARLY
            for l in range(SIDE // LANES):
                lanes = pl.ds(l * LANES, LANES)
                gain = [spread[s, pl.ds(t, 1), lanes] for t in range(BINS)]
                for c in range(SIDE // ROWS):
                    rows = pl.ds(c * ROWS, ROWS)
                    acc = jnp.zeros((ROWS, LANES), F32)
                    for t in range(BINS):
                        acc += trips[s, t, rows, lanes].astype(F32) * anchor_fit[t, rows, :] * gain[t]
                    part[s, rows, lanes] = acc
            for h in range(2):
                halves(s, h).start()

        @pl.when(k == SLOTS - EARLY + LAG)
        def _():
            for copy in swaps:
                copy.wait_recv()

        @pl.when((k >= SLOTS - EARLY + LAG) & (k < SLOTS + LAG))
        def _():
            s = k - LAG - (SLOTS - EARLY)
            for h in range(2):
                shipped(s, h).wait_recv()
                rows = pl.ds(kept64[h], 64)
                for l in range(SIDE // LANES):
                    lanes = pl.ds(l * LANES, LANES)
                    acc = jnp.zeros((64, LANES), F32)
                    for t in range(BINS):
                        fit = trips[s, t, rows, lanes].astype(F32) * anchor_fit[t, rows, :]
                        acc += fit * spread[s, pl.ds(t, 1), lanes]
                        acc += ship_in[s, h, t, :, lanes] * peer[h, s, pl.ds(t, 1), lanes]
                    part[s, rows, lanes] = acc
                quarters(s, h).start()

        @pl.when((k >= LAG) & (k < SLOTS - EARLY + LAG))
        def _():
            s = k - LAG + EARLY
            for h in range(2):
                halves(s, h).wait_recv()
                part[s, pl.ds(kept64[h], 64), :] += half_in[s, h]
                quarters(s, h).start()

        @pl.when((k >= 2 * LAG) & (k < SLOTS + 2 * LAG))
        def _():
            s = lax.rem(k - 2 * LAG + EARLY, SLOTS)
            dead = jnp.where(cols_ref[s] >= 0, 0.0, 1.0).astype(F32)
            for h in range(2):
                quarters(s, h).wait_recv()
                rows = pl.ds(kept32[h], 32)
                daily = part[s, rows, :] + quarter_in[s, h]
                factor[s, rows, :] = target[h, s].astype(F32) / (daily + dead)
                back(s, h).start()

        @pl.when((k >= 3 * LAG) & (k < SLOTS + 3 * LAG))
        def _():
            s = lax.rem(k - 3 * LAG + EARLY, SLOTS)
            for h in range(2):
                back(s, h).wait_recv()
                whole(s, h).start()

        @pl.when(k >= 4 * LAG)
        def _():
            s = lax.rem(k - 4 * LAG + EARLY, SLOTS)
            for h in range(2):
                whole(s, h).wait_recv()
            for t in range(BINS):
                for l in range(SIDE // LANES):
                    lanes = pl.ds(l * LANES, LANES)
                    gain = spread[s, pl.ds(t, 1), lanes]
                    acc = jnp.zeros((ROWS, LANES), F32)
                    for c in range(SIDE // ROWS):
                        rows = pl.ds(c * ROWS, ROWS)
                        value = trips[s, t, rows, lanes].astype(F32) * anchor_fit[t, rows, :] * factor[s, rows, lanes]
                        acc += value
                        trips[s, t, rows, lanes] = (value * gain).astype(jnp.bfloat16)
                    sums[s, pl.ds(t, 1), lanes] = jnp.sum(acc, axis=0, keepdims=True) * gain
            store_fitted(s).start()

    total, more = owner_sums(wide2, wide2_in, narrow2, narrow2_in, wide2_sem, narrow2_s, narrow2_r, lambda: None)
    pending += more
    gap = total / dest8[used, :] - 1.0
    for t in range(BINS):
        for b in range(2):
            gap_ref[pl.ds(t, 1), pl.ds(b * SIDE, SIDE)] = gap[2 * t + b : 2 * t + b + 1, :]

    for copy in pending:
        copy.wait_send()

    @pl.loop(0, EARLY)
    def _(s):
        for h in range(2):
            shipped(s, h).wait_send()

    @pl.loop(EARLY, SLOTS)
    def _(s):
        for h in range(2):
            halves(s, h).wait_send()

    @pl.loop(0, SLOTS)
    def _(s):
        for h in range(2):
            quarters(s, h).wait_send()
            back(s, h).wait_send()
            whole(s, h).wait_send()
        store_fitted(s).wait()


def on_device(trip_counts, anchor_hour, dest_hour, daily_target, block_columns):
    vmem = lambda *shape: pltpu.VMEM(shape, F32)
    dma = lambda *shape: pltpu.SemaphoreType.DMA(shape)
    scratch = [
        pltpu.VMEM((SLOTS, BINS, SIDE, SIDE), jnp.bfloat16),
        vmem(SLOTS, SIDE, SIDE),
        vmem(SLOTS, SIDE, SIDE),
        vmem(SLOTS, 2, 64, SIDE),
        vmem(SLOTS, 2, 32, SIDE),
        pltpu.VMEM((2, SLOTS, 32, SIDE), jnp.bfloat16),
        vmem(BINS, SIDE, LANES),
        vmem(BINS, SIDE, LANES),
        vmem(BINS, 512),
        vmem(8, SIDE),
        pltpu.VMEM((2, CHIPS * OWN, KEYS), BF16),
        pltpu.VMEM((2, KEYS, CHIPS * OWN), BF16),
        vmem(KEYS // 8, 8, SIDE),
        vmem(KEYS // 8, 8, SIDE),
        vmem(2, CHIPS, OWN, SIDE),
    ] + [vmem(CHIPS, OWN, SIDE), vmem(CHIPS, OWN, SIDE), vmem(CHIPS, OWN, SIDE), vmem(CHIPS - 1, OWN, SIDE)] * 2 + [
        vmem(EARLY, 2, BINS, 64, SIDE),
        vmem(EARLY, 2, BINS, 64, SIDE),
        vmem(2, EARLY, 8, SIDE),
        dma(SLOTS), dma(2), pltpu.SemaphoreType.DMA, dma(SLOTS),
    ] + [dma(SLOTS, 2)] * 8 + [dma(2), dma(CHIPS - 1), dma(CHIPS - 1)] * 3 + [dma(EARLY, 2)] * 2 + [dma(2)] * 2
    fitted, gap = pl.pallas_call(
        kernel,
        out_shape=(
            jax.ShapeDtypeStruct(trip_counts.shape, jnp.bfloat16),
            jax.ShapeDtypeStruct((BINS, 512), F32),
        ),
        in_specs=[
            pl.BlockSpec(memory_space=pltpu.SMEM),
            pl.BlockSpec(memory_space=pltpu.VMEM),
            pl.BlockSpec(memory_space=pl.ANY),
            pl.BlockSpec(memory_space=pl.ANY),
            pl.BlockSpec(memory_space=pl.ANY),
        ],
        out_specs=(pl.BlockSpec(memory_space=pl.ANY), pl.BlockSpec(memory_space=pltpu.VMEM)),
        scratch_shapes=scratch,
        compiler_params=pltpu.CompilerParams(
            collective_id=0, has_side_effects=True, vmem_limit_bytes=40 * 1024 * 1024
        ),
        cost_estimate=pl.CostEstimate(flops=40_000_000, bytes_accessed=11_000_000, transcendentals=0),
    )(*[pltpu.with_memory_space_constraint(a, pltpu.HBM) for a in (block_columns, anchor_hour, trip_counts, dest_hour, daily_target)])
    return fitted, gap


def solution(mesh):
    placed = (
        P("tm", "orig", None, None),
        P("tm", "orig"),
        P("tm", None),
        P("orig", None, None),
        P("orig"),
    )
    return jax.shard_map(
        on_device,
        mesh=mesh,
        in_specs=placed,
        out_specs=(P("tm", "orig", None, None), P("tm", "orig")),
        check_vma=False,
    )
```

```python
import jax
import jax.numpy as jnp
from jax import lax
from jax.experimental import pallas as pl
from jax.experimental.pallas import tpu as pltpu
from jax.sharding import PartitionSpec as P

BINS = 3
SLOTS = 12
SIDE = 256
LANES = 128
CHIPS_Z, CHIPS_Y = 8, 4
CHIPS = CHIPS_Z * CHIPS_Y
OWN = 8
USED = 2 * BINS
KEYS = 128
ROWS = 64
EARLY = 4
FIRST = 4
AT_ONCE = 1
LAG = 2
F32 = jnp.float32
BF16 = jnp.bfloat16


def picked(onehot, values):
    high = values.astype(BF16)
    rest = values - high.astype(F32)
    middle = rest.astype(BF16)
    low = (rest - middle.astype(F32)).astype(BF16)
    return sum(jnp.dot(onehot, part, preferred_element_type=F32) for part in (low, middle, high))


def hops(offset):
    return min(offset[0], CHIPS_Z - offset[0]) + min(offset[1], CHIPS_Y - offset[1])


OFFSETS = sorted(
    [(a, b) for a in range(CHIPS_Z) for b in range(CHIPS_Y) if (a, b) != (0, 0)], key=hops, reverse=True
)


def send(src, dst, send_sem, recv_sem, tm, orig):
    return pltpu.make_async_remote_copy(
        src_ref=src,
        dst_ref=dst,
        send_sem=send_sem,
        recv_sem=recv_sem,
        device_id=(tm, orig),
        device_id_type=pl.DeviceIdType.MESH,
    )


def kernel(
    cols_ref, anchor_ref, trips_ref, dest_ref, target_ref,
    fitted_ref, gap_ref,
    trips, part, factor, half_in, quarter_in, target, row_acc, anchor_fit, dest_row, dest8,
    onehot, by_key, sums, spread, gains, wide, wide_in, narrow, narrow_in,
    wide2, wide2_in, narrow2, narrow2_in, ship, ship_in, peer, col_out, col_in,
    trips_sem, target_sem, dest_sem, fitted_sem,
    half_s, half_r, quarter_s, quarter_r, back_s, back_r, whole_s, whole_r,
    wide_sem, narrow_s, narrow_r, gain_sem, gain_s, gain_r, wide2_sem, narrow2_s, narrow2_r,
    ship_s, ship_r, peer_s, peer_r, col_s, col_r,
):
    x = lax.axis_index("tm")
    q = lax.axis_index("orig")
    chip, core = q // 2, q % 2
    z, y = chip // CHIPS_Y, chip % CHIPS_Y
    v = x // 2
    u = (x + v) % 2
    pa = x + 1 - 2 * (x % 2)
    pb = 3 - x
    other = chip * 2 + 1 - core
    chips = [((z + a) % CHIPS_Z) * CHIPS_Y + (y + b) % CHIPS_Y for a, b in OFFSETS]

    barrier = pltpu.get_barrier_semaphore()
    partners = [(x, 2 * o + core) for o in chips] + [(x, other), (pa, q), (pb, q)]
    for t_, o_ in partners:
        pl.semaphore_signal(barrier, inc=1, device_id=(t_, o_), device_id_type=pl.DeviceIdType.MESH)

    first, second = (pa, pb), (pb, pa)
    keep1, keep2 = (u, v), (v, u)
    kept64 = [pl.multiple_of(128 * h + 64 * keep1[h], 64) for h in range(2)]
    sent64 = [pl.multiple_of(128 * h + 64 * (1 - keep1[h]), 64) for h in range(2)]
    kept32 = [pl.multiple_of(kept64[h] + 32 * keep2[h], 32) for h in range(2)]
    sent32 = [pl.multiple_of(kept64[h] + 32 * (1 - keep2[h]), 32) for h in range(2)]

    def load_trips(s):
        return pltpu.make_async_copy(trips_ref.at[:, s], trips.at[s], trips_sem.at[s])

    def load_target(h):
        return pltpu.make_async_copy(
            target_ref.at[:, pl.ds(kept32[h], 32), :], target.at[h], target_sem.at[h]
        )

    load_dest = pltpu.make_async_copy(
        dest_ref.at[:, pl.ds(pl.multiple_of(q * 512, 512), 512)], dest_row, dest_sem
    )

    @pl.loop(0, SLOTS)
    def _(s):
        load_trips(s).start()

    load_dest.start()
    for h in range(2):
        load_target(h).start()

    r = lax.broadcasted_iota(jnp.int32, (2 * CHIPS * OWN, KEYS), 0)
    block = 4 * ((r >> 3) & (CHIPS - 1)) + 2 * (r >> 8) + (r & 1)
    row_key = jnp.where((r & 7) < 2 * BINS, block * BINS + ((r & 7) >> 1), -2)
    lane = lax.broadcasted_iota(jnp.int32, (1, KEYS), 1)
    key = jnp.full((1, KEYS), -1, jnp.int32)
    for s in range(SLOTS):
        col = cols_ref[s]
        in_slot = (lane >= 8 * s) & (lane < 8 * s + BINS) & (jnp.full((1, KEYS), col, jnp.int32) >= 0)
        key = jnp.where(in_slot, col * BINS + lane - 8 * s, key)
    match = jnp.where(row_key == key, 1.0, 0.0).astype(F32)
    for c in range(2):
        half = match[c * CHIPS * OWN : (c + 1) * CHIPS * OWN, :]
        onehot[c] = half.astype(BF16)
        by_key[c] = half.T.astype(BF16)

    diagonal = lax.broadcasted_iota(jnp.int32, (SIDE, SIDE), 0) == lax.broadcasted_iota(
        jnp.int32, (SIDE, SIDE), 1
    )
    row_acc[...] = jnp.zeros_like(row_acc)
    sums[...] = jnp.zeros_like(sums)
    gains[...] = jnp.zeros_like(gains)
    dest8[...] = jnp.ones_like(dest8)

    @pl.loop(0, SLOTS)
    def _(s):
        load_trips(s).wait()
        live = jnp.where(cols_ref[s] >= 0, 1.0, 0.0).astype(F32)
        for t in range(BINS):
            for c in range(SIDE // ROWS):
                rows = pl.ds(c * ROWS, ROWS)
                left = trips[s, t, rows, pl.ds(0, LANES)].astype(F32)
                right = trips[s, t, rows, pl.ds(LANES, LANES)].astype(F32)
                row_acc[t, rows, :] += (left + right) * live

    for t in range(BINS):
        hour = jnp.sum(jnp.where(diagonal, anchor_ref[pl.ds(t, 1), :], 0.0), axis=1, keepdims=True)
        total = jnp.sum(row_acc[t], axis=1, keepdims=True)
        anchor_fit[t] = jnp.broadcast_to(hour / total, (SIDE, LANES))

    @pl.loop(0, SLOTS)
    def _(s):
        for t in range(BINS):
            for l in range(SIDE // LANES):
                lanes = pl.ds(l * LANES, LANES)
                acc = jnp.zeros((ROWS, LANES), F32)
                for c in range(SIDE // ROWS):
                    rows = pl.ds(c * ROWS, ROWS)
                    acc += trips[s, t, rows, lanes].astype(F32) * anchor_fit[t, rows, :]
                sums[s, pl.ds(t, 1), lanes] = jnp.sum(acc, axis=0, keepdims=True)

    def shipped(s, h):
        return send(ship.at[s, h], ship_in.at[s, h], ship_s.at[s, h], ship_r.at[s, h], first[h], q)

    def fill_early(s):
        for h in range(2):
            rows = pl.ds(sent64[h], 64)
            for t in range(BINS):
                for l in range(SIDE // LANES):
                    lanes = pl.ds(l * LANES, LANES)
                    ship[s, h, t, :, lanes] = trips[s, t, rows, lanes].astype(F32) * anchor_fit[t, rows, :]

    def send_early(s):
        for h in range(2):
            shipped(s, h).start()

    def later_early():
        @pl.loop(AT_ONCE, EARLY)
        def _(s):
            fill_early(s)
            send_early(s)

    pl.loop(0, AT_ONCE)(fill_early)
    pl.semaphore_wait(barrier, len(partners))
    pl.loop(0, AT_ONCE)(send_early)

    used = pl.ds(0, USED)

    def owner_sums(wide, wide_in, narrow, narrow_in, wide_sem, narrow_s, narrow_r, meanwhile):
        def by_owner(c):
            return picked(onehot[c], sums[...].reshape(KEYS, SIDE)).reshape(CHIPS, OWN, SIDE)

        wide[...] = by_owner(1 - core)
        copies = [send(wide, wide_in, wide_sem.at[0], wide_sem.at[1], x, other)]
        copies[0].start()
        kept = by_owner(core)
        copies[0].wait_recv()
        narrow[...] = kept + wide_in[...]
        for i, o in enumerate(chips):
            copies.append(send(narrow.at[o, used, :], narrow_in.at[i, used, :], narrow_s.at[i], narrow_r.at[i], x, 2 * o + core))
            copies[-1].start()
        meanwhile()
        total = narrow[chip, used, :]
        for i in reversed(range(len(chips))):
            copies[1 + i].wait_recv()
            total = total + narrow_in[i, used, :]
        return total, copies

    load_dest.wait()
    for t in range(BINS):
        for b in range(2):
            dest8[pl.ds(2 * t + b, 1), :] = dest_row[pl.ds(t, 1), pl.ds(b * SIDE, SIDE)]

    total, pending = owner_sums(wide, wide_in, narrow, narrow_in, wide_sem, narrow_s, narrow_r, later_early)
    gains[core, chip, used, :] = dest8[used, :] / jnp.maximum(total, 1.0)
    copies = []
    for i, o in enumerate(chips):
        mine = gains.at[core, chip, used, :]
        copies.append(send(mine, mine, gain_s.at[i], gain_r.at[i], x, 2 * o + core))
        copies[-1].start()
    for copy in copies:
        copy.wait_recv()
    swap = send(gains.at[core], gains.at[core], gain_sem.at[0], gain_sem.at[1], x, other)
    swap.start()

    def by_slot(c):
        return picked(by_key[c], gains[c].reshape(CHIPS * OWN, SIDE)).reshape(KEYS // 8, 8, SIDE)

    near = by_slot(core)
    swap.wait_recv()
    spread[...] = near + by_slot(1 - core)
    pending += copies + [swap]
    early_slots = pl.ds(0, EARLY)
    swaps = [
        send(spread.at[early_slots], peer.at[h], peer_s.at[h], peer_r.at[h], first[h], q) for h in range(2)
    ]
    for copy in swaps:
        copy.start()
    pending += swaps
    for h in range(2):
        load_target(h).wait()

    def halves(s, h):
        return send(
            part.at[s, pl.ds(sent64[h], 64), :], half_in.at[s, h], half_s.at[s, h], half_r.at[s, h], first[h], q
        )

    def quarters(s, h):
        return send(
            part.at[s, pl.ds(sent32[h], 32), :], quarter_in.at[s, h], quarter_s.at[s, h], quarter_r.at[s, h], second[h], q
        )

    def back(s, h):
        rows = pl.ds(kept32[h], 32)
        return send(factor.at[s, rows, :], factor.at[s, rows, :], back_s.at[s, h], back_r.at[s, h], second[h], q)

    def whole(s, h):
        rows = pl.ds(kept64[h], 64)
        return send(factor.at[s, rows, :], factor.at[s, rows, :], whole_s.at[s, h], whole_r.at[s, h], first[h], q)

    def columns(s, h):
        rows = pl.ds(0, BINS)
        return send(
            col_out.at[s, h, rows, :], col_in.at[s, h, rows, :], col_s.at[s, h], col_r.at[s, h], first[h], q
        )

    def store_fitted(s):
        return pltpu.make_async_copy(trips.at[s], fitted_ref.at[:, s], fitted_sem.at[s])

    def finish(s, with_sums):
        for h in range(2):
            whole(s, h).wait_recv()
        for t in range(BINS):
            for l in range(SIDE // LANES):
                lanes = pl.ds(l * LANES, LANES)
                gain = spread[s, pl.ds(t, 1), lanes]
                acc = jnp.zeros((ROWS, LANES), F32)
                for c in range(SIDE // ROWS):
                    rows = pl.ds(c * ROWS, ROWS)
                    value = trips[s, t, rows, lanes].astype(F32) * anchor_fit[t, rows, :] * factor[s, rows, lanes]
                    acc += value
                    trips[s, t, rows, lanes] = (value * gain).astype(jnp.bfloat16)
                if with_sums:
                    sums[s, pl.ds(t, 1), lanes] = jnp.sum(acc, axis=0, keepdims=True) * gain
        store_fitted(s).start()

    def finish_early():
        @pl.loop(0, EARLY)
        def _(s):
            finish(s, False)

    def early_at(p):
        return (p >= FIRST) & (p < FIRST + EARLY)

    def later_at(p):
        return ((p >= 0) & (p < FIRST)) | ((p >= FIRST + EARLY) & (p < SLOTS))

    def slot_at(p):
        return jnp.where(p < FIRST, p + EARLY, jnp.where(p < FIRST + EARLY, p - FIRST, p))

    @pl.loop(0, SLOTS + 4 * LAG)
    def _(k):
        @pl.when(later_at(k))
        def _():
            s = slot_at(k)
            for l in range(SIDE // LANES):
                lanes = pl.ds(l * LANES, LANES)
                gain = [spread[s, pl.ds(t, 1), lanes] for t in range(BINS)]
                for c in range(SIDE // ROWS):
                    rows = pl.ds(c * ROWS, ROWS)
                    acc = jnp.zeros((ROWS, LANES), F32)
                    for t in range(BINS):
                        acc += trips[s, t, rows, lanes].astype(F32) * anchor_fit[t, rows, :] * gain[t]
                    part[s, rows, lanes] = acc
            for h in range(2):
                halves(s, h).start()

        @pl.when(k == FIRST + LAG)
        def _():
            for copy in swaps:
                copy.wait_recv()

        @pl.when(early_at(k - LAG))
        def _():
            s = slot_at(k - LAG)
            for h in range(2):
                shipped(s, h).wait_recv()
                rows = pl.ds(kept64[h], 64)
                for l in range(SIDE // LANES):
                    lanes = pl.ds(l * LANES, LANES)
                    acc = jnp.zeros((64, LANES), F32)
                    for t in range(BINS):
                        fit = trips[s, t, rows, lanes].astype(F32) * anchor_fit[t, rows, :]
                        acc += fit * spread[s, pl.ds(t, 1), lanes]
                        acc += ship_in[s, h, t, :, lanes] * peer[h, s, pl.ds(t, 1), lanes]
                    part[s, rows, lanes] = acc
                quarters(s, h).start()

        @pl.when(later_at(k - LAG))
        def _():
            s = slot_at(k - LAG)
            for h in range(2):
                halves(s, h).wait_recv()
                part[s, pl.ds(kept64[h], 64), :] += half_in[s, h]
                quarters(s, h).start()

        @pl.when((k >= 2 * LAG) & (k < SLOTS + 2 * LAG))
        def _():
            s = slot_at(k - 2 * LAG)
            dead = jnp.where(cols_ref[s] >= 0, 0.0, 1.0).astype(F32)
            for h in range(2):
                quarters(s, h).wait_recv()
                rows = pl.ds(kept32[h], 32)
                daily = part[s, rows, :] + quarter_in[s, h]
                factor[s, rows, :] = target[h, s].astype(F32) / (daily + dead)
                back(s, h).start()

        @pl.when(later_at(k - 3 * LAG))
        def _():
            s = slot_at(k - 3 * LAG)
            for h in range(2):
                back(s, h).wait_recv()
                whole(s, h).start()

        @pl.when(early_at(k - 3 * LAG))
        def _():
            s = slot_at(k - 3 * LAG)
            for h in range(2):
                back(s, h).wait_recv()
            for t in range(BINS):
                for l in range(SIDE // LANES):
                    lanes = pl.ds(l * LANES, LANES)
                    own = jnp.zeros((64, LANES), F32)
                    for h in range(2):
                        rows = pl.ds(kept64[h], 64)
                        ratio = factor[s, rows, lanes]
                        own += trips[s, t, rows, lanes].astype(F32) * anchor_fit[t, rows, :] * ratio
                        total = jnp.sum(ship_in[s, h, t, :, lanes] * ratio, axis=0, keepdims=True)
                        col_out[s, h, pl.ds(t, 1), lanes] = total * peer[h, s, pl.ds(t, 1), lanes]
                    total = jnp.sum(own, axis=0, keepdims=True)
                    sums[s, pl.ds(t, 1), lanes] = total * spread[s, pl.ds(t, 1), lanes]
            for h in range(2):
                columns(s, h).start()

        @pl.when(later_at(k - 4 * LAG))
        def _():
            finish(slot_at(k - 4 * LAG), True)

        @pl.when(early_at(k - 4 * LAG))
        def _():
            s = slot_at(k - 4 * LAG)
            rows = pl.ds(0, BINS)
            for h in range(2):
                columns(s, h).wait_recv()
                sums[s, rows, :] += col_in[s, h, rows, :]

    @pl.loop(0, EARLY)
    def _(s):
        for h in range(2):
            whole(s, h).start()

    total, more = owner_sums(wide2, wide2_in, narrow2, narrow2_in, wide2_sem, narrow2_s, narrow2_r, finish_early)
    pending += more
    gap = total / dest8[used, :] - 1.0
    for t in range(BINS):
        for b in range(2):
            gap_ref[pl.ds(t, 1), pl.ds(b * SIDE, SIDE)] = gap[2 * t + b : 2 * t + b + 1, :]

    for copy in pending:
        copy.wait_send()

    @pl.loop(0, EARLY)
    def _(s):
        for h in range(2):
            shipped(s, h).wait_send()
            columns(s, h).wait_send()

    @pl.loop(EARLY, SLOTS)
    def _(s):
        for h in range(2):
            halves(s, h).wait_send()

    @pl.loop(0, SLOTS)
    def _(s):
        for h in range(2):
            quarters(s, h).wait_send()
            back(s, h).wait_send()
            whole(s, h).wait_send()
        store_fitted(s).wait()


def on_device(trip_counts, anchor_hour, dest_hour, daily_target, block_columns):
    vmem = lambda *shape: pltpu.VMEM(shape, F32)
    dma = lambda *shape: pltpu.SemaphoreType.DMA(shape)
    scratch = [
        pltpu.VMEM((SLOTS, BINS, SIDE, SIDE), jnp.bfloat16),
        vmem(SLOTS, SIDE, SIDE),
        vmem(SLOTS, SIDE, SIDE),
        vmem(SLOTS, 2, 64, SIDE),
        vmem(SLOTS, 2, 32, SIDE),
        pltpu.VMEM((2, SLOTS, 32, SIDE), jnp.bfloat16),
        vmem(BINS, SIDE, LANES),
        vmem(BINS, SIDE, LANES),
        vmem(BINS, 512),
        vmem(8, SIDE),
        pltpu.VMEM((2, CHIPS * OWN, KEYS), BF16),
        pltpu.VMEM((2, KEYS, CHIPS * OWN), BF16),
        vmem(KEYS // 8, 8, SIDE),
        vmem(KEYS // 8, 8, SIDE),
        vmem(2, CHIPS, OWN, SIDE),
    ] + [vmem(CHIPS, OWN, SIDE), vmem(CHIPS, OWN, SIDE), vmem(CHIPS, OWN, SIDE), vmem(CHIPS - 1, OWN, SIDE)] * 2 + [
        vmem(EARLY, 2, BINS, 64, SIDE),
        vmem(EARLY, 2, BINS, 64, SIDE),
        vmem(2, EARLY, 8, SIDE),
        vmem(EARLY, 2, 8, SIDE),
        vmem(EARLY, 2, 8, SIDE),
        dma(SLOTS), dma(2), pltpu.SemaphoreType.DMA, dma(SLOTS),
    ] + [dma(SLOTS, 2)] * 8 + [dma(2), dma(CHIPS - 1), dma(CHIPS - 1)] * 3 + [dma(EARLY, 2)] * 2 + [dma(2)] * 2 + [dma(EARLY, 2)] * 2
    fitted, gap = pl.pallas_call(
        kernel,
        out_shape=(
            jax.ShapeDtypeStruct(trip_counts.shape, jnp.bfloat16),
            jax.ShapeDtypeStruct((BINS, 512), F32),
        ),
        in_specs=[
            pl.BlockSpec(memory_space=pltpu.SMEM),
            pl.BlockSpec(memory_space=pltpu.VMEM),
            pl.BlockSpec(memory_space=pl.ANY),
            pl.BlockSpec(memory_space=pl.ANY),
            pl.BlockSpec(memory_space=pl.ANY),
        ],
        out_specs=(pl.BlockSpec(memory_space=pl.ANY), pl.BlockSpec(memory_space=pltpu.VMEM)),
        scratch_shapes=scratch,
        compiler_params=pltpu.CompilerParams(
            collective_id=0, has_side_effects=True, vmem_limit_bytes=40 * 1024 * 1024
        ),
        cost_estimate=pl.CostEstimate(flops=40_000_000, bytes_accessed=11_000_000, transcendentals=0),
    )(*[pltpu.with_memory_space_constraint(a, pltpu.HBM) for a in (block_columns, anchor_hour, trip_counts, dest_hour, daily_target)])
    return fitted, gap


def solution(mesh):
    placed = (
        P("tm", "orig", None, None),
        P("tm", "orig"),
        P("tm", None),
        P("orig", None, None),
        P("orig"),
    )
    return jax.shard_map(
        on_device,
        mesh=mesh,
        in_specs=placed,
        out_specs=(P("tm", "orig", None, None), P("tm", "orig")),
        check_vma=False,
    )
```

```python
import jax
import jax.numpy as jnp
from jax import lax
from jax.experimental import pallas as pl
from jax.experimental.pallas import tpu as pltpu
from jax.sharding import PartitionSpec as P

BINS = 3
SLOTS = 12
SIDE = 256
LANES = 128
CHIPS_Z, CHIPS_Y = 8, 4
CHIPS = CHIPS_Z * CHIPS_Y
OWN = 8
USED = 2 * BINS
KEYS = 128
ROWS = 64
EARLY = 4
FIRST = 4
AT_ONCE = 1
LAG = 3
F32 = jnp.float32
BF16 = jnp.bfloat16


def picked(onehot, values):
    high = values.astype(BF16)
    rest = values - high.astype(F32)
    middle = rest.astype(BF16)
    low = (rest - middle.astype(F32)).astype(BF16)
    return sum(jnp.dot(onehot, part, preferred_element_type=F32) for part in (low, middle, high))


def hops(offset):
    return min(offset[0], CHIPS_Z - offset[0]) + min(offset[1], CHIPS_Y - offset[1])


OFFSETS = sorted(
    [(a, b) for a in range(CHIPS_Z) for b in range(CHIPS_Y) if (a, b) != (0, 0)], key=hops, reverse=True
)


def send(src, dst, send_sem, recv_sem, tm, orig):
    return pltpu.make_async_remote_copy(
        src_ref=src,
        dst_ref=dst,
        send_sem=send_sem,
        recv_sem=recv_sem,
        device_id=(tm, orig),
        device_id_type=pl.DeviceIdType.MESH,
    )


def kernel(
    cols_ref, anchor_ref, trips_ref, dest_ref, target_ref,
    fitted_ref, gap_ref,
    trips, part, factor, half_in, quarter_in, target, row_acc, anchor_fit, dest_row, dest8,
    onehot, by_key, sums, spread, gains, wide, wide_in, narrow, narrow_in,
    wide2, wide2_in, narrow2, narrow2_in, ship, ship_in, peer, col_out, col_in,
    trips_sem, target_sem, dest_sem, fitted_sem,
    half_s, half_r, quarter_s, quarter_r, back_s, back_r, whole_s, whole_r,
    wide_sem, narrow_s, narrow_r, gain_sem, gain_s, gain_r, wide2_sem, narrow2_s, narrow2_r,
    ship_s, ship_r, peer_s, peer_r, col_s, col_r,
):
    x = lax.axis_index("tm")
    q = lax.axis_index("orig")
    chip, core = q // 2, q % 2
    z, y = chip // CHIPS_Y, chip % CHIPS_Y
    v = x // 2
    u = (x + v) % 2
    pa = x + 1 - 2 * (x % 2)
    pb = 3 - x
    other = chip * 2 + 1 - core
    chips = [((z + a) % CHIPS_Z) * CHIPS_Y + (y + b) % CHIPS_Y for a, b in OFFSETS]

    barrier = pltpu.get_barrier_semaphore()
    partners = [(x, 2 * o + core) for o in chips] + [(x, other), (pa, q), (pb, q)]
    for t_, o_ in partners:
        pl.semaphore_signal(barrier, inc=1, device_id=(t_, o_), device_id_type=pl.DeviceIdType.MESH)

    first, second = (pa, pb), (pb, pa)
    keep1, keep2 = (u, v), (v, u)
    kept64 = [pl.multiple_of(128 * h + 64 * keep1[h], 64) for h in range(2)]
    sent64 = [pl.multiple_of(128 * h + 64 * (1 - keep1[h]), 64) for h in range(2)]
    kept32 = [pl.multiple_of(kept64[h] + 32 * keep2[h], 32) for h in range(2)]
    sent32 = [pl.multiple_of(kept64[h] + 32 * (1 - keep2[h]), 32) for h in range(2)]

    def load_trips(s):
        return pltpu.make_async_copy(trips_ref.at[:, s], trips.at[s], trips_sem.at[s])

    def load_target(h):
        return pltpu.make_async_copy(
            target_ref.at[:, pl.ds(kept32[h], 32), :], target.at[h], target_sem.at[h]
        )

    load_dest = pltpu.make_async_copy(
        dest_ref.at[:, pl.ds(pl.multiple_of(q * 512, 512), 512)], dest_row, dest_sem
    )

    @pl.loop(0, SLOTS)
    def _(s):
        load_trips(s).start()

    load_dest.start()
    for h in range(2):
        load_target(h).start()

    r = lax.broadcasted_iota(jnp.int32, (2 * CHIPS * OWN, KEYS), 0)
    block = 4 * ((r >> 3) & (CHIPS - 1)) + 2 * (r >> 8) + (r & 1)
    row_key = jnp.where((r & 7) < 2 * BINS, block * BINS + ((r & 7) >> 1), -2)
    lane = lax.broadcasted_iota(jnp.int32, (1, KEYS), 1)
    key = jnp.full((1, KEYS), -1, jnp.int32)
    for s in range(SLOTS):
        col = cols_ref[s]
        in_slot = (lane >= 8 * s) & (lane < 8 * s + BINS) & (jnp.full((1, KEYS), col, jnp.int32) >= 0)
        key = jnp.where(in_slot, col * BINS + lane - 8 * s, key)
    match = jnp.where(row_key == key, 1.0, 0.0).astype(F32)
    for c in range(2):
        half = match[c * CHIPS * OWN : (c + 1) * CHIPS * OWN, :]
        onehot[c] = half.astype(BF16)
        by_key[c] = half.T.astype(BF16)

    diagonal = lax.broadcasted_iota(jnp.int32, (SIDE, SIDE), 0) == lax.broadcasted_iota(
        jnp.int32, (SIDE, SIDE), 1
    )
    row_acc[...] = jnp.zeros_like(row_acc)
    sums[...] = jnp.zeros_like(sums)
    gains[...] = jnp.zeros_like(gains)
    dest8[...] = jnp.ones_like(dest8)

    @pl.loop(0, SLOTS)
    def _(s):
        load_trips(s).wait()
        live = jnp.where(cols_ref[s] >= 0, 1.0, 0.0).astype(F32)
        for t in range(BINS):
            for c in range(SIDE // ROWS):
                rows = pl.ds(c * ROWS, ROWS)
                left = trips[s, t, rows, pl.ds(0, LANES)].astype(F32)
                right = trips[s, t, rows, pl.ds(LANES, LANES)].astype(F32)
                row_acc[t, rows, :] += (left + right) * live

    for t in range(BINS):
        hour = jnp.sum(jnp.where(diagonal, anchor_ref[pl.ds(t, 1), :], 0.0), axis=1, keepdims=True)
        total = jnp.sum(row_acc[t], axis=1, keepdims=True)
        anchor_fit[t] = jnp.broadcast_to(hour / total, (SIDE, LANES))

    @pl.loop(0, SLOTS)
    def _(s):
        for t in range(BINS):
            for l in range(SIDE // LANES):
                lanes = pl.ds(l * LANES, LANES)
                acc = jnp.zeros((ROWS, LANES), F32)
                for c in range(SIDE // ROWS):
                    rows = pl.ds(c * ROWS, ROWS)
                    acc += trips[s, t, rows, lanes].astype(F32) * anchor_fit[t, rows, :]
                sums[s, pl.ds(t, 1), lanes] = jnp.sum(acc, axis=0, keepdims=True)

    def shipped(s, h):
        return send(ship.at[s, h], ship_in.at[s, h], ship_s.at[s, h], ship_r.at[s, h], first[h], q)

    def fill_early(s):
        for h in range(2):
            rows = pl.ds(sent64[h], 64)
            for t in range(BINS):
                for l in range(SIDE // LANES):
                    lanes = pl.ds(l * LANES, LANES)
                    ship[s, h, t, :, lanes] = trips[s, t, rows, lanes].astype(F32) * anchor_fit[t, rows, :]

    def send_early(s):
        for h in range(2):
            shipped(s, h).start()

    def later_early():
        @pl.loop(AT_ONCE, EARLY)
        def _(s):
            fill_early(s)
            send_early(s)

    pl.loop(0, AT_ONCE)(fill_early)
    def by_owner(c):
        return picked(onehot[c], sums[...].reshape(KEYS, SIDE)).reshape(CHIPS, OWN, SIDE)

    wide[...] = by_owner(1 - core)
    narrow[...] = by_owner(core)
    pl.semaphore_wait(barrier, len(partners))
    pl.loop(0, AT_ONCE)(send_early)

    used = pl.ds(0, USED)

    def owner_sums(wide, wide_in, narrow, narrow_in, wide_sem, narrow_s, narrow_r, beside, meanwhile):
        copies = [send(wide, wide_in, wide_sem.at[0], wide_sem.at[1], x, other)]
        copies[0].start()
        beside()
        copies[0].wait_recv()
        narrow[...] += wide_in[...]
        for i, o in enumerate(chips):
            copies.append(send(narrow.at[o, used, :], narrow_in.at[i, used, :], narrow_s.at[i], narrow_r.at[i], x, 2 * o + core))
            copies[-1].start()
        meanwhile()
        total = narrow[chip, used, :]
        for i in reversed(range(len(chips))):
            copies[1 + i].wait_recv()
            total = total + narrow_in[i, used, :]
        return total, copies

    load_dest.wait()
    for t in range(BINS):
        for b in range(2):
            dest8[pl.ds(2 * t + b, 1), :] = dest_row[pl.ds(t, 1), pl.ds(b * SIDE, SIDE)]

    total, pending = owner_sums(wide, wide_in, narrow, narrow_in, wide_sem, narrow_s, narrow_r, lambda: None, later_early)
    gains[core, chip, used, :] = dest8[used, :] / jnp.maximum(total, 1.0)
    copies = []
    for i, o in enumerate(chips):
        mine = gains.at[core, chip, used, :]
        copies.append(send(mine, mine, gain_s.at[i], gain_r.at[i], x, 2 * o + core))
        copies[-1].start()
    for copy in copies:
        copy.wait_recv()
    swap = send(gains.at[core], gains.at[core], gain_sem.at[0], gain_sem.at[1], x, other)
    swap.start()

    def by_slot(c):
        return picked(by_key[c], gains[c].reshape(CHIPS * OWN, SIDE)).reshape(KEYS // 8, 8, SIDE)

    near = by_slot(core)
    swap.wait_recv()
    spread[...] = near + by_slot(1 - core)
    pending += copies + [swap]
    early_slots = pl.ds(0, EARLY)
    swaps = [
        send(spread.at[early_slots], peer.at[h], peer_s.at[h], peer_r.at[h], first[h], q) for h in range(2)
    ]
    for copy in swaps:
        copy.start()
    pending += swaps
    for h in range(2):
        load_target(h).wait()

    def halves(s, h):
        return send(
            part.at[s, pl.ds(sent64[h], 64), :], half_in.at[s, h], half_s.at[s, h], half_r.at[s, h], first[h], q
        )

    def quarters(s, h):
        return send(
            part.at[s, pl.ds(sent32[h], 32), :], quarter_in.at[s, h], quarter_s.at[s, h], quarter_r.at[s, h], second[h], q
        )

    def back(s, h):
        rows = pl.ds(kept32[h], 32)
        return send(factor.at[s, rows, :], factor.at[s, rows, :], back_s.at[s, h], back_r.at[s, h], second[h], q)

    def whole(s, h):
        rows = pl.ds(kept64[h], 64)
        return send(factor.at[s, rows, :], factor.at[s, rows, :], whole_s.at[s, h], whole_r.at[s, h], first[h], q)

    def columns(s, h):
        rows = pl.ds(0, BINS)
        return send(
            col_out.at[s, h, rows, :], col_in.at[s, h, rows, :], col_s.at[s, h], col_r.at[s, h], first[h], q
        )

    def store_fitted(s):
        return pltpu.make_async_copy(trips.at[s], fitted_ref.at[:, s], fitted_sem.at[s])

    def finish(s, with_sums):
        for h in range(2):
            whole(s, h).wait_recv()
        for t in range(BINS):
            for l in range(SIDE // LANES):
                lanes = pl.ds(l * LANES, LANES)
                gain = spread[s, pl.ds(t, 1), lanes]
                acc = jnp.zeros((ROWS, LANES), F32)
                for c in range(SIDE // ROWS):
                    rows = pl.ds(c * ROWS, ROWS)
                    value = trips[s, t, rows, lanes].astype(F32) * anchor_fit[t, rows, :] * factor[s, rows, lanes]
                    acc += value
                    trips[s, t, rows, lanes] = (value * gain).astype(jnp.bfloat16)
                if with_sums:
                    sums[s, pl.ds(t, 1), lanes] = jnp.sum(acc, axis=0, keepdims=True) * gain
        store_fitted(s).start()

    def finish_early():
        @pl.loop(0, EARLY)
        def _(s):
            finish(s, False)

    def early_at(p):
        return (p >= FIRST) & (p < FIRST + EARLY)

    def later_at(p):
        return ((p >= 0) & (p < FIRST)) | ((p >= FIRST + EARLY) & (p < SLOTS))

    def slot_at(p):
        return jnp.where(p < FIRST, p + EARLY, jnp.where(p < FIRST + EARLY, p - FIRST, p))

    @pl.loop(0, SLOTS + 4 * LAG)
    def _(k):
        @pl.when(later_at(k))
        def _():
            s = slot_at(k)
            for l in range(SIDE // LANES):
                lanes = pl.ds(l * LANES, LANES)
                gain = [spread[s, pl.ds(t, 1), lanes] for t in range(BINS)]
                for c in range(SIDE // ROWS):
                    rows = pl.ds(c * ROWS, ROWS)
                    acc = jnp.zeros((ROWS, LANES), F32)
                    for t in range(BINS):
                        acc += trips[s, t, rows, lanes].astype(F32) * anchor_fit[t, rows, :] * gain[t]
                    part[s, rows, lanes] = acc
            for h in range(2):
                halves(s, h).start()

        @pl.when(k == FIRST + LAG)
        def _():
            for copy in swaps:
                copy.wait_recv()

        @pl.when(early_at(k - LAG))
        def _():
            s = slot_at(k - LAG)
            for h in range(2):
                shipped(s, h).wait_recv()
                rows = pl.ds(kept64[h], 64)
                for l in range(SIDE // LANES):
                    lanes = pl.ds(l * LANES, LANES)
                    acc = jnp.zeros((64, LANES), F32)
                    for t in range(BINS):
                        fit = trips[s, t, rows, lanes].astype(F32) * anchor_fit[t, rows, :]
                        acc += fit * spread[s, pl.ds(t, 1), lanes]
                        acc += ship_in[s, h, t, :, lanes] * peer[h, s, pl.ds(t, 1), lanes]
                    part[s, rows, lanes] = acc
                quarters(s, h).start()

        @pl.when(later_at(k - LAG))
        def _():
            s = slot_at(k - LAG)
            for h in range(2):
                halves(s, h).wait_recv()
                part[s, pl.ds(kept64[h], 64), :] += half_in[s, h]
                quarters(s, h).start()

        @pl.when((k >= 2 * LAG) & (k < SLOTS + 2 * LAG))
        def _():
            s = slot_at(k - 2 * LAG)
            dead = jnp.where(cols_ref[s] >= 0, 0.0, 1.0).astype(F32)
            for h in range(2):
                quarters(s, h).wait_recv()
                rows = pl.ds(kept32[h], 32)
                daily = part[s, rows, :] + quarter_in[s, h]
                factor[s, rows, :] = target[h, s].astype(F32) / (daily + dead)
                back(s, h).start()

        @pl.when(later_at(k - 3 * LAG))
        def _():
            s = slot_at(k - 3 * LAG)
            for h in range(2):
                back(s, h).wait_recv()
                whole(s, h).start()

        @pl.when(early_at(k - 3 * LAG))
        def _():
            s = slot_at(k - 3 * LAG)
            for h in range(2):
                back(s, h).wait_recv()
            for t in range(BINS):
                for l in range(SIDE // LANES):
                    lanes = pl.ds(l * LANES, LANES)
                    own = jnp.zeros((64, LANES), F32)
                    for h in range(2):
                        rows = pl.ds(kept64[h], 64)
                        ratio = factor[s, rows, lanes]
                        own += trips[s, t, rows, lanes].astype(F32) * anchor_fit[t, rows, :] * ratio
                        total = jnp.sum(ship_in[s, h, t, :, lanes] * ratio, axis=0, keepdims=True)
                        col_out[s, h, pl.ds(t, 1), lanes] = total * peer[h, s, pl.ds(t, 1), lanes]
                    total = jnp.sum(own, axis=0, keepdims=True)
                    sums[s, pl.ds(t, 1), lanes] = total * spread[s, pl.ds(t, 1), lanes]
            for h in range(2):
                columns(s, h).start()

        @pl.when(later_at(k - 4 * LAG))
        def _():
            finish(slot_at(k - 4 * LAG), True)

        @pl.when(early_at(k - 4 * LAG))
        def _():
            s = slot_at(k - 4 * LAG)
            rows = pl.ds(0, BINS)
            for h in range(2):
                columns(s, h).wait_recv()
                sums[s, rows, :] += col_in[s, h, rows, :]

    @pl.loop(0, EARLY)
    def _(s):
        for h in range(2):
            whole(s, h).start()

    wide2[...] = by_owner(1 - core)

    def near_product():
        narrow2[...] = by_owner(core)

    total, more = owner_sums(wide2, wide2_in, narrow2, narrow2_in, wide2_sem, narrow2_s, narrow2_r, near_product, finish_early)
    pending += more
    gap = total / dest8[used, :] - 1.0
    for t in range(BINS):
        for b in range(2):
            gap_ref[pl.ds(t, 1), pl.ds(b * SIDE, SIDE)] = gap[2 * t + b : 2 * t + b + 1, :]

    for copy in pending:
        copy.wait_send()

    @pl.loop(0, EARLY)
    def _(s):
        for h in range(2):
            shipped(s, h).wait_send()
            columns(s, h).wait_send()

    @pl.loop(EARLY, SLOTS)
    def _(s):
        for h in range(2):
            halves(s, h).wait_send()

    @pl.loop(0, SLOTS)
    def _(s):
        for h in range(2):
            quarters(s, h).wait_send()
            back(s, h).wait_send()
            whole(s, h).wait_send()
        store_fitted(s).wait()


def on_device(trip_counts, anchor_hour, dest_hour, daily_target, block_columns):
    vmem = lambda *shape: pltpu.VMEM(shape, F32)
    dma = lambda *shape: pltpu.SemaphoreType.DMA(shape)
    scratch = [
        pltpu.VMEM((SLOTS, BINS, SIDE, SIDE), jnp.bfloat16),
        vmem(SLOTS, SIDE, SIDE),
        vmem(SLOTS, SIDE, SIDE),
        vmem(SLOTS, 2, 64, SIDE),
        vmem(SLOTS, 2, 32, SIDE),
        pltpu.VMEM((2, SLOTS, 32, SIDE), jnp.bfloat16),
        vmem(BINS, SIDE, LANES),
        vmem(BINS, SIDE, LANES),
        vmem(BINS, 512),
        vmem(8, SIDE),
        pltpu.VMEM((2, CHIPS * OWN, KEYS), BF16),
        pltpu.VMEM((2, KEYS, CHIPS * OWN), BF16),
        vmem(KEYS // 8, 8, SIDE),
        vmem(KEYS // 8, 8, SIDE),
        vmem(2, CHIPS, OWN, SIDE),
    ] + [vmem(CHIPS, OWN, SIDE), vmem(CHIPS, OWN, SIDE), vmem(CHIPS, OWN, SIDE), vmem(CHIPS - 1, OWN, SIDE)] * 2 + [
        vmem(EARLY, 2, BINS, 64, SIDE),
        vmem(EARLY, 2, BINS, 64, SIDE),
        vmem(2, EARLY, 8, SIDE),
        vmem(EARLY, 2, 8, SIDE),
        vmem(EARLY, 2, 8, SIDE),
        dma(SLOTS), dma(2), pltpu.SemaphoreType.DMA, dma(SLOTS),
    ] + [dma(SLOTS, 2)] * 8 + [dma(2), dma(CHIPS - 1), dma(CHIPS - 1)] * 3 + [dma(EARLY, 2)] * 2 + [dma(2)] * 2 + [dma(EARLY, 2)] * 2
    fitted, gap = pl.pallas_call(
        kernel,
        out_shape=(
            jax.ShapeDtypeStruct(trip_counts.shape, jnp.bfloat16),
            jax.ShapeDtypeStruct((BINS, 512), F32),
        ),
        in_specs=[
            pl.BlockSpec(memory_space=pltpu.SMEM),
            pl.BlockSpec(memory_space=pltpu.VMEM),
            pl.BlockSpec(memory_space=pl.ANY),
            pl.BlockSpec(memory_space=pl.ANY),
            pl.BlockSpec(memory_space=pl.ANY),
        ],
        out_specs=(pl.BlockSpec(memory_space=pl.ANY), pl.BlockSpec(memory_space=pltpu.VMEM)),
        scratch_shapes=scratch,
        compiler_params=pltpu.CompilerParams(
            collective_id=0, has_side_effects=True, vmem_limit_bytes=40 * 1024 * 1024
        ),
        cost_estimate=pl.CostEstimate(flops=40_000_000, bytes_accessed=11_000_000, transcendentals=0),
    )(*[pltpu.with_memory_space_constraint(a, pltpu.HBM) for a in (block_columns, anchor_hour, trip_counts, dest_hour, daily_target)])
    return fitted, gap


def solution(mesh):
    placed = (
        P("tm", "orig", None, None),
        P("tm", "orig"),
        P("tm", None),
        P("orig", None, None),
        P("orig"),
    )
    return jax.shard_map(
        on_device,
        mesh=mesh,
        in_specs=placed,
        out_specs=(P("tm", "orig", None, None), P("tm", "orig")),
        check_vma=False,
    )
```

```python
import jax
import jax.numpy as jnp
from jax import lax
from jax.experimental import pallas as pl
from jax.experimental.pallas import tpu as pltpu
from jax.sharding import PartitionSpec as P

BINS = 3
SLOTS = 12
SIDE = 256
LANES = 128
CHIPS_Z, CHIPS_Y = 8, 4
CHIPS = CHIPS_Z * CHIPS_Y
OWN = 8
USED = 2 * BINS
KEYS = 128
ROWS = 64
EARLY = 4
FIRST = 4
AT_ONCE = 1
LAG = 3
F32 = jnp.float32
BF16 = jnp.bfloat16


def picked(onehot, values):
    high = values.astype(BF16)
    rest = values - high.astype(F32)
    middle = rest.astype(BF16)
    low = (rest - middle.astype(F32)).astype(BF16)
    return sum(jnp.dot(onehot, part, preferred_element_type=F32) for part in (low, middle, high))


def hops(offset):
    return min(offset[0], CHIPS_Z - offset[0]) + min(offset[1], CHIPS_Y - offset[1])


OFFSETS = sorted(
    [(a, b) for a in range(CHIPS_Z) for b in range(CHIPS_Y) if (a, b) != (0, 0)], key=hops, reverse=True
)


def send(src, dst, send_sem, recv_sem, tm, orig):
    return pltpu.make_async_remote_copy(
        src_ref=src,
        dst_ref=dst,
        send_sem=send_sem,
        recv_sem=recv_sem,
        device_id=(tm, orig),
        device_id_type=pl.DeviceIdType.MESH,
    )


def kernel(
    cols_ref, anchor_ref, trips_ref, dest_ref, target_ref,
    fitted_ref, gap_ref,
    trips, part, factor, half_in, quarter_in, target, row_acc, anchor_fit, dest_row, dest8,
    onehot, by_key, sums, spread, gains, wide, wide_in, narrow, narrow_in,
    wide2, wide2_in, narrow2, narrow2_in, ship, ship_in, peer, col_out, col_in,
    trips_sem, target_sem, dest_sem, fitted_sem,
    half_s, half_r, quarter_s, quarter_r, back_s, back_r, whole_s, whole_r,
    wide_sem, narrow_s, narrow_r, gain_sem, gain_s, gain_r, wide2_sem, narrow2_s, narrow2_r,
    ship_s, ship_r, peer_s, peer_r, col_s, col_r,
):
    x = lax.axis_index("tm")
    q = lax.axis_index("orig")
    chip, core = q // 2, q % 2
    z, y = chip // CHIPS_Y, chip % CHIPS_Y
    v = x // 2
    u = (x + v) % 2
    pa = x + 1 - 2 * (x % 2)
    pb = 3 - x
    other = chip * 2 + 1 - core
    chips = [((z + a) % CHIPS_Z) * CHIPS_Y + (y + b) % CHIPS_Y for a, b in OFFSETS]

    barrier = pltpu.get_barrier_semaphore()
    partners = [(x, 2 * o + core) for o in chips] + [(x, other), (pa, q), (pb, q)]
    for t_, o_ in partners:
        pl.semaphore_signal(barrier, inc=1, device_id=(t_, o_), device_id_type=pl.DeviceIdType.MESH)

    first, second = (pa, pb), (pb, pa)
    keep1, keep2 = (u, v), (v, u)
    kept64 = [pl.multiple_of(128 * h + 64 * keep1[h], 64) for h in range(2)]
    sent64 = [pl.multiple_of(128 * h + 64 * (1 - keep1[h]), 64) for h in range(2)]
    kept32 = [pl.multiple_of(kept64[h] + 32 * keep2[h], 32) for h in range(2)]
    sent32 = [pl.multiple_of(kept64[h] + 32 * (1 - keep2[h]), 32) for h in range(2)]

    def load_trips(s):
        return pltpu.make_async_copy(trips_ref.at[:, s], trips.at[s], trips_sem.at[s])

    def load_target(h):
        return pltpu.make_async_copy(
            target_ref.at[:, pl.ds(kept32[h], 32), :], target.at[h], target_sem.at[h]
        )

    load_dest = pltpu.make_async_copy(
        dest_ref.at[:, pl.ds(pl.multiple_of(q * 512, 512), 512)], dest_row, dest_sem
    )

    @pl.loop(0, SLOTS)
    def _(s):
        load_trips(s).start()

    load_dest.start()
    for h in range(2):
        load_target(h).start()

    r = lax.broadcasted_iota(jnp.int32, (2 * CHIPS * OWN, KEYS), 0)
    block = 4 * ((r >> 3) & (CHIPS - 1)) + 2 * (r >> 8) + (r & 1)
    row_key = jnp.where((r & 7) < 2 * BINS, block * BINS + ((r & 7) >> 1), -2)
    lane = lax.broadcasted_iota(jnp.int32, (1, KEYS), 1)
    key = jnp.full((1, KEYS), -1, jnp.int32)
    for s in range(SLOTS):
        col = cols_ref[s]
        in_slot = (lane >= 8 * s) & (lane < 8 * s + BINS) & (jnp.full((1, KEYS), col, jnp.int32) >= 0)
        key = jnp.where(in_slot, col * BINS + lane - 8 * s, key)
    match = jnp.where(row_key == key, 1.0, 0.0).astype(F32)
    for c in range(2):
        half = match[c * CHIPS * OWN : (c + 1) * CHIPS * OWN, :]
        onehot[c] = half.astype(BF16)
        by_key[c] = half.T.astype(BF16)

    diagonal = lax.broadcasted_iota(jnp.int32, (SIDE, SIDE), 0) == lax.broadcasted_iota(
        jnp.int32, (SIDE, SIDE), 1
    )
    row_acc[...] = jnp.zeros_like(row_acc)
    sums[...] = jnp.zeros_like(sums)
    gains[...] = jnp.zeros_like(gains)
    dest8[...] = jnp.ones_like(dest8)

    @pl.loop(0, SLOTS)
    def _(s):
        load_trips(s).wait()
        live = jnp.where(cols_ref[s] >= 0, 1.0, 0.0).astype(F32)
        for t in range(BINS):
            for c in range(SIDE // ROWS):
                rows = pl.ds(c * ROWS, ROWS)
                left = trips[s, t, rows, pl.ds(0, LANES)].astype(F32)
                right = trips[s, t, rows, pl.ds(LANES, LANES)].astype(F32)
                row_acc[t, rows, :] += (left + right) * live

    for t in range(BINS):
        hour = jnp.sum(jnp.where(diagonal, anchor_ref[pl.ds(t, 1), :], 0.0), axis=1, keepdims=True)
        total = jnp.sum(row_acc[t], axis=1, keepdims=True)
        anchor_fit[t] = jnp.broadcast_to(hour / total, (SIDE, LANES))

    @pl.loop(0, SLOTS)
    def _(s):
        for t in range(BINS):
            for l in range(SIDE // LANES):
                lanes = pl.ds(l * LANES, LANES)
                acc = jnp.zeros((ROWS, LANES), F32)
                for c in range(SIDE // ROWS):
                    rows = pl.ds(c * ROWS, ROWS)
                    acc += trips[s, t, rows, lanes].astype(F32) * anchor_fit[t, rows, :]
                sums[s, pl.ds(t, 1), lanes] = jnp.sum(acc, axis=0, keepdims=True)

    def shipped(s, h):
        return send(ship.at[s, h], ship_in.at[s, h], ship_s.at[s, h], ship_r.at[s, h], first[h], q)

    def fill_early(s):
        for h in range(2):
            rows = pl.ds(sent64[h], 64)
            for t in range(BINS):
                for l in range(SIDE // LANES):
                    lanes = pl.ds(l * LANES, LANES)
                    ship[s, h, t, :, lanes] = trips[s, t, rows, lanes].astype(F32) * anchor_fit[t, rows, :]

    def send_early(s):
        for h in range(2):
            shipped(s, h).start()

    def later_early():
        @pl.loop(AT_ONCE, EARLY)
        def _(s):
            send_early(s)

    pl.loop(0, EARLY)(fill_early)
    def by_owner(c):
        return picked(onehot[c], sums[...].reshape(KEYS, SIDE)).reshape(CHIPS, OWN, SIDE)

    wide[...] = by_owner(1 - core)
    narrow[...] = by_owner(core)
    pl.semaphore_wait(barrier, len(partners))
    pl.loop(0, AT_ONCE)(send_early)

    used = pl.ds(0, USED)

    def owner_sums(wide, wide_in, narrow, narrow_in, wide_sem, narrow_s, narrow_r, beside, meanwhile):
        copies = [send(wide, wide_in, wide_sem.at[0], wide_sem.at[1], x, other)]
        copies[0].start()
        beside()
        copies[0].wait_recv()
        narrow[...] += wide_in[...]
        for i, o in enumerate(chips):
            copies.append(send(narrow.at[o, used, :], narrow_in.at[i, used, :], narrow_s.at[i], narrow_r.at[i], x, 2 * o + core))
            copies[-1].start()
        meanwhile()
        total = narrow[chip, used, :]
        for i in reversed(range(len(chips))):
            copies[1 + i].wait_recv()
            total = total + narrow_in[i, used, :]
        return total, copies

    load_dest.wait()
    for t in range(BINS):
        for b in range(2):
            dest8[pl.ds(2 * t + b, 1), :] = dest_row[pl.ds(t, 1), pl.ds(b * SIDE, SIDE)]

    total, pending = owner_sums(wide, wide_in, narrow, narrow_in, wide_sem, narrow_s, narrow_r, lambda: None, later_early)
    gains[core, chip, used, :] = dest8[used, :] / jnp.maximum(total, 1.0)
    copies = []
    for i, o in enumerate(chips):
        mine = gains.at[core, chip, used, :]
        copies.append(send(mine, mine, gain_s.at[i], gain_r.at[i], x, 2 * o + core))
        copies[-1].start()
    for copy in copies:
        copy.wait_recv()
    swap = send(gains.at[core], gains.at[core], gain_sem.at[0], gain_sem.at[1], x, other)
    swap.start()

    def by_slot(c):
        return picked(by_key[c], gains[c].reshape(CHIPS * OWN, SIDE)).reshape(KEYS // 8, 8, SIDE)

    near = by_slot(core)
    swap.wait_recv()
    spread[...] = near + by_slot(1 - core)
    pending += copies + [swap]
    early_slots = pl.ds(0, EARLY)
    swaps = [
        send(spread.at[early_slots], peer.at[h], peer_s.at[h], peer_r.at[h], first[h], q) for h in range(2)
    ]
    for copy in swaps:
        copy.start()
    pending += swaps
    for h in range(2):
        load_target(h).wait()

    def halves(s, h):
        return send(
            part.at[s, pl.ds(sent64[h], 64), :], half_in.at[s, h], half_s.at[s, h], half_r.at[s, h], first[h], q
        )

    def quarters(s, h):
        return send(
            part.at[s, pl.ds(sent32[h], 32), :], quarter_in.at[s, h], quarter_s.at[s, h], quarter_r.at[s, h], second[h], q
        )

    def back(s, h):
        rows = pl.ds(kept32[h], 32)
        return send(factor.at[s, rows, :], factor.at[s, rows, :], back_s.at[s, h], back_r.at[s, h], second[h], q)

    def whole(s, h):
        rows = pl.ds(kept64[h], 64)
        return send(factor.at[s, rows, :], factor.at[s, rows, :], whole_s.at[s, h], whole_r.at[s, h], first[h], q)

    def columns(s, h):
        rows = pl.ds(0, BINS)
        return send(
            col_out.at[s, h, rows, :], col_in.at[s, h, rows, :], col_s.at[s, h], col_r.at[s, h], first[h], q
        )

    def store_fitted(s):
        return pltpu.make_async_copy(trips.at[s], fitted_ref.at[:, s], fitted_sem.at[s])

    def finish(s, with_sums):
        for h in range(2):
            whole(s, h).wait_recv()
        for t in range(BINS):
            for l in range(SIDE // LANES):
                lanes = pl.ds(l * LANES, LANES)
                gain = spread[s, pl.ds(t, 1), lanes]
                acc = jnp.zeros((ROWS, LANES), F32)
                for c in range(SIDE // ROWS):
                    rows = pl.ds(c * ROWS, ROWS)
                    value = trips[s, t, rows, lanes].astype(F32) * anchor_fit[t, rows, :] * factor[s, rows, lanes]
                    acc += value
                    trips[s, t, rows, lanes] = (value * gain).astype(jnp.bfloat16)
                if with_sums:
                    sums[s, pl.ds(t, 1), lanes] = jnp.sum(acc, axis=0, keepdims=True) * gain
        store_fitted(s).start()

    def finish_early():
        @pl.loop(0, EARLY)
        def _(s):
            finish(s, False)

    def early_at(p):
        return (p >= FIRST) & (p < FIRST + EARLY)

    def later_at(p):
        return ((p >= 0) & (p < FIRST)) | ((p >= FIRST + EARLY) & (p < SLOTS))

    def slot_at(p):
        return jnp.where(p < FIRST, p + EARLY, jnp.where(p < FIRST + EARLY, p - FIRST, p))

    @pl.loop(0, SLOTS + 4 * LAG)
    def _(k):
        @pl.when(later_at(k))
        def _():
            s = slot_at(k)
            for l in range(SIDE // LANES):
                lanes = pl.ds(l * LANES, LANES)
                gain = [spread[s, pl.ds(t, 1), lanes] for t in range(BINS)]
                for c in range(SIDE // ROWS):
                    rows = pl.ds(c * ROWS, ROWS)
                    acc = jnp.zeros((ROWS, LANES), F32)
                    for t in range(BINS):
                        acc += trips[s, t, rows, lanes].astype(F32) * anchor_fit[t, rows, :] * gain[t]
                    part[s, rows, lanes] = acc
            for h in range(2):
                halves(s, h).start()

        @pl.when(k == FIRST + LAG)
        def _():
            for copy in swaps:
                copy.wait_recv()

        @pl.when(early_at(k - LAG))
        def _():
            s = slot_at(k - LAG)
            for h in range(2):
                shipped(s, h).wait_recv()
                rows = pl.ds(kept64[h], 64)
                for l in range(SIDE // LANES):
                    lanes = pl.ds(l * LANES, LANES)
                    acc = jnp.zeros((64, LANES), F32)
                    for t in range(BINS):
                        fit = trips[s, t, rows, lanes].astype(F32) * anchor_fit[t, rows, :]
                        acc += fit * spread[s, pl.ds(t, 1), lanes]
                        acc += ship_in[s, h, t, :, lanes] * peer[h, s, pl.ds(t, 1), lanes]
                    part[s, rows, lanes] = acc
                quarters(s, h).start()

        @pl.when(later_at(k - LAG))
        def _():
            s = slot_at(k - LAG)
            for h in range(2):
                halves(s, h).wait_recv()
                part[s, pl.ds(kept64[h], 64), :] += half_in[s, h]
                quarters(s, h).start()

        @pl.when((k >= 2 * LAG) & (k < SLOTS + 2 * LAG))
        def _():
            s = slot_at(k - 2 * LAG)
            dead = jnp.where(cols_ref[s] >= 0, 0.0, 1.0).astype(F32)
            for h in range(2):
                quarters(s, h).wait_recv()
                rows = pl.ds(kept32[h], 32)
                daily = part[s, rows, :] + quarter_in[s, h]
                factor[s, rows, :] = target[h, s].astype(F32) / (daily + dead)
                back(s, h).start()

        @pl.when(later_at(k - 3 * LAG))
        def _():
            s = slot_at(k - 3 * LAG)
            for h in range(2):
                back(s, h).wait_recv()
                whole(s, h).start()

        @pl.when(early_at(k - 3 * LAG))
        def _():
            s = slot_at(k - 3 * LAG)
            for h in range(2):
                back(s, h).wait_recv()
            for t in range(BINS):
                for l in range(SIDE // LANES):
                    lanes = pl.ds(l * LANES, LANES)
                    own = jnp.zeros((64, LANES), F32)
                    for h in range(2):
                        rows = pl.ds(kept64[h], 64)
                        ratio = factor[s, rows, lanes]
                        own += trips[s, t, rows, lanes].astype(F32) * anchor_fit[t, rows, :] * ratio
                        total = jnp.sum(ship_in[s, h, t, :, lanes] * ratio, axis=0, keepdims=True)
                        col_out[s, h, pl.ds(t, 1), lanes] = total * peer[h, s, pl.ds(t, 1), lanes]
                    total = jnp.sum(own, axis=0, keepdims=True)
                    sums[s, pl.ds(t, 1), lanes] = total * spread[s, pl.ds(t, 1), lanes]
            for h in range(2):
                columns(s, h).start()

        @pl.when(later_at(k - 4 * LAG))
        def _():
            finish(slot_at(k - 4 * LAG), True)

        @pl.when(early_at(k - 4 * LAG))
        def _():
            s = slot_at(k - 4 * LAG)
            rows = pl.ds(0, BINS)
            for h in range(2):
                columns(s, h).wait_recv()
                sums[s, rows, :] += col_in[s, h, rows, :]

    @pl.loop(0, EARLY)
    def _(s):
        for h in range(2):
            whole(s, h).start()

    wide2[...] = by_owner(1 - core)

    def near_product():
        narrow2[...] = by_owner(core)

    total, more = owner_sums(wide2, wide2_in, narrow2, narrow2_in, wide2_sem, narrow2_s, narrow2_r, near_product, finish_early)
    pending += more
    gap = total / dest8[used, :] - 1.0
    for t in range(BINS):
        for b in range(2):
            gap_ref[pl.ds(t, 1), pl.ds(b * SIDE, SIDE)] = gap[2 * t + b : 2 * t + b + 1, :]

    for copy in pending:
        copy.wait_send()

    @pl.loop(0, EARLY)
    def _(s):
        for h in range(2):
            shipped(s, h).wait_send()
            columns(s, h).wait_send()

    @pl.loop(EARLY, SLOTS)
    def _(s):
        for h in range(2):
            halves(s, h).wait_send()

    @pl.loop(0, SLOTS)
    def _(s):
        for h in range(2):
            quarters(s, h).wait_send()
            back(s, h).wait_send()
            whole(s, h).wait_send()
        store_fitted(s).wait()


def on_device(trip_counts, anchor_hour, dest_hour, daily_target, block_columns):
    vmem = lambda *shape: pltpu.VMEM(shape, F32)
    dma = lambda *shape: pltpu.SemaphoreType.DMA(shape)
    scratch = [
        pltpu.VMEM((SLOTS, BINS, SIDE, SIDE), jnp.bfloat16),
        vmem(SLOTS, SIDE, SIDE),
        vmem(SLOTS, SIDE, SIDE),
        vmem(SLOTS, 2, 64, SIDE),
        vmem(SLOTS, 2, 32, SIDE),
        pltpu.VMEM((2, SLOTS, 32, SIDE), jnp.bfloat16),
        vmem(BINS, SIDE, LANES),
        vmem(BINS, SIDE, LANES),
        vmem(BINS, 512),
        vmem(8, SIDE),
        pltpu.VMEM((2, CHIPS * OWN, KEYS), BF16),
        pltpu.VMEM((2, KEYS, CHIPS * OWN), BF16),
        vmem(KEYS // 8, 8, SIDE),
        vmem(KEYS // 8, 8, SIDE),
        vmem(2, CHIPS, OWN, SIDE),
    ] + [vmem(CHIPS, OWN, SIDE), vmem(CHIPS, OWN, SIDE), vmem(CHIPS, OWN, SIDE), vmem(CHIPS - 1, OWN, SIDE)] * 2 + [
        vmem(EARLY, 2, BINS, 64, SIDE),
        vmem(EARLY, 2, BINS, 64, SIDE),
        vmem(2, EARLY, 8, SIDE),
        vmem(EARLY, 2, 8, SIDE),
        vmem(EARLY, 2, 8, SIDE),
        dma(SLOTS), dma(2), pltpu.SemaphoreType.DMA, dma(SLOTS),
    ] + [dma(SLOTS, 2)] * 8 + [dma(2), dma(CHIPS - 1), dma(CHIPS - 1)] * 3 + [dma(EARLY, 2)] * 2 + [dma(2)] * 2 + [dma(EARLY, 2)] * 2
    fitted, gap = pl.pallas_call(
        kernel,
        out_shape=(
            jax.ShapeDtypeStruct(trip_counts.shape, jnp.bfloat16),
            jax.ShapeDtypeStruct((BINS, 512), F32),
        ),
        in_specs=[
            pl.BlockSpec(memory_space=pltpu.SMEM),
            pl.BlockSpec(memory_space=pltpu.VMEM),
            pl.BlockSpec(memory_space=pl.ANY),
            pl.BlockSpec(memory_space=pl.ANY),
            pl.BlockSpec(memory_space=pl.ANY),
        ],
        out_specs=(pl.BlockSpec(memory_space=pl.ANY), pl.BlockSpec(memory_space=pltpu.VMEM)),
        scratch_shapes=scratch,
        compiler_params=pltpu.CompilerParams(
            collective_id=0, has_side_effects=True, vmem_limit_bytes=40 * 1024 * 1024
        ),
        cost_estimate=pl.CostEstimate(flops=40_000_000, bytes_accessed=11_000_000, transcendentals=0),
    )(*[pltpu.with_memory_space_constraint(a, pltpu.HBM) for a in (block_columns, anchor_hour, trip_counts, dest_hour, daily_target)])
    return fitted, gap


def solution(mesh):
    placed = (
        P("tm", "orig", None, None),
        P("tm", "orig"),
        P("tm", None),
        P("orig", None, None),
        P("orig"),
    )
    return jax.shard_map(
        on_device,
        mesh=mesh,
        in_specs=placed,
        out_specs=(P("tm", "orig", None, None), P("tm", "orig")),
        check_vma=False,
    )
```
